32 devices in a mesh: gx: 2 (over x), gy: 4 (over z), gz: 4 (over y, core).
Axes of the slice: x: 2, y: 2, z: 4, core: 2. Of those that a mesh axis runs over, the one named last changes fastest.
Arguments:
- field: bfloat16 [32, 6, 32, 512], P(None, 'gx', 'gy', 'gz'), may hold values from -6 to 6
- cotangent: bfloat16 [32, 6, 32, 512], P(None, 'gx', 'gy', 'gz'), may hold values from -6 to 6
- cosmology: float32 [2], replicated, may hold values from -1 to 1
- lift_weight: float32 [2, 256], replicated, may hold values from -4 to 4
- lift_bias: float32 [256], replicated, may hold values from -3 to 3
- style_weight: float32 [256, 32], replicated, may hold values from -0.375 to 0.375
- style_bias: float32 [32], replicated, may hold values from -2 to 2
- kernel: float32 [32, 32, 3, 3, 3], replicated, may hold values from -0.21875 to 0.21875
- offset: float32 [32], replicated, may hold values from -3 to 3
Outputs:
- grad_field: bfloat16 [32, 6, 32, 512], P(None, 'gx', 'gy', 'gz')
- grad_kernel: float32 [32, 32, 3, 3, 3], replicated
- grad_offset: float32 [32], replicated
- grad_lift: float32 [2, 256], replicated
- grad_liftbias: float32 [256], replicated
- grad_style: float32 [256, 32], replicated
- grad_stylebias: float32 [32], replicated
The draws below stay inside these ranges and needn't reach their ends.
All inputs are finite; a program needn't handle non-finite values.
Results may differ from the reference program's by a relative error of at most 0.013.
Values may be sent and summed in bfloat16 or wider, within the bound.
A program may use at most 64 MiB of HBM per device.

```python
import jax
import jax.numpy as jnp
from jax import lax

C = 32
HID = 256
NPAR = 2
CX = 3
NX = 6
NY = 32
NZ = 512


def steps_of(key, shape, split, smallest, largest):
    level = 1.0
    for axis_at, shards_of in split:
        steps = jax.random.uniform(jax.random.fold_in(jax.random.fold_in(key, 6), axis_at), (shards_of,), jnp.float32, smallest / len(split), largest / len(split))
        level = level * jnp.repeat(jnp.exp(steps), shape[axis_at] // shards_of).reshape((-1,) + (1,) * (len(shape) - 1 - axis_at))
    return level


def normal_values(own_key, shape, spread, limit, cuts=(), kind=jnp.bfloat16):
    array = spread * jax.random.normal(own_key, shape, jnp.float32)
    if cuts:
        array = array * steps_of(own_key, shape, cuts, -0.22, 0.18)
    return jnp.clip(array, -limit, limit).astype(kind)


def setup_inputs(seed: int = 0) -> dict:
    arg_keys = jax.random.split(jax.random.key(seed), 10)
    field = normal_values(arg_keys[0], (C, NX, NY, NZ), 1.0, 6.0, ((1, 2), (2, 4), (3, 4)))
    cotangent = normal_values(arg_keys[1], (C, NX, NY, NZ), 1.0, 6.0, ((1, 2), (2, 4), (3, 4)))
    cosmology = jnp.clip(jax.random.uniform(arg_keys[2], (NPAR,), jnp.float32, -1.0, 1.0), -1.0, 1.0)
    lift_weight = normal_values(arg_keys[3], (NPAR, HID), NPAR ** -0.5, 4.0, (), jnp.float32)
    lift_bias = normal_values(arg_keys[4], (HID,), 0.5, 3.0, (), jnp.float32)
    style_weight = normal_values(arg_keys[5], (HID, C), HID ** -0.5, 0.375, (), jnp.float32)
    style_bias = normal_values(arg_keys[6], (C,), 0.3, 2.0, (), jnp.float32)
    kernel = normal_values(arg_keys[7], (C, C, 3, 3, 3), (C * 27) ** -0.5, 0.21875, (), jnp.float32)
    offset = normal_values(arg_keys[8], (C,), 0.5, 3.0, (), jnp.float32)
    return {"field": field, "cotangent": cotangent, "cosmology": cosmology, "lift_weight": lift_weight, "lift_bias": lift_bias, "style_weight": style_weight, "style_bias": style_bias, "kernel": kernel, "offset": offset}


demod_eps = 1e-06
clip_eps = 1e-06

def silu_slope(values):
    logistic = jax.nn.sigmoid(values)
    return logistic * (1.0 + values * (1.0 - logistic))

def modulate(cosmology, lift_weight, lift_bias, style_weight, style_bias, kernel):
    lifted = jnp.dot(cosmology[None, :], lift_weight, precision=lax.Precision.HIGHEST)[0] + lift_bias
    hidden = jax.nn.silu(lifted)
    styles = jnp.dot(hidden[None, :], style_weight, precision=lax.Precision.HIGHEST)[0] + style_bias + 1.0
    modded = kernel * styles[None, :, None, None, None]
    inv_norm = lax.rsqrt(lax.optimization_barrier(jnp.sum(modded * modded, axis=(1, 2, 3, 4))) + demod_eps)
    scaled = (modded * inv_norm[:, None, None, None, None]).astype(jnp.bfloat16)
    return (lifted, hidden, styles, modded, inv_norm, scaled)

def param_backward(sums_kernel, sums_offset, cosmology, style_weight, kernel, lifted, hidden, styles, modded, inv_norm):
    projected = lax.optimization_barrier(jnp.sum(sums_kernel * modded, axis=(1, 2, 3, 4)))
    mod_grad = inv_norm[:, None, None, None, None] * (sums_kernel - modded * (inv_norm * inv_norm * projected)[:, None, None, None, None])
    kernel_raw = mod_grad * styles[None, :, None, None, None]
    styles_grad = lax.optimization_barrier(jnp.sum(mod_grad * kernel, axis=(0, 2, 3, 4)))
    hidden_grad = jnp.dot(style_weight, styles_grad[:, None], precision=lax.Precision.HIGHEST)[:, 0]
    lifted_grad = hidden_grad * silu_slope(lifted)
    style_raw = hidden[:, None] * styles_grad[None, :]
    lift_raw = cosmology[:, None] * lifted_grad[None, :]
    members = (kernel_raw, sums_offset, lift_raw, lifted_grad, style_raw, styles_grad)
    square_sum = sum((jnp.sum(member * member) for member in members))
    entries = sum((member.size for member in members))
    factor = jnp.minimum(1.0, lax.rsqrt(square_sum / entries + clip_eps))
    return tuple((factor * member for member in members))

def conv_valid(operand, filters):
    return lax.conv_general_dilated(operand[None].astype(jnp.float32), filters.astype(jnp.float32), (1, 1, 1), 'VALID', dimension_numbers=('NCDHW', 'OIDHW', 'NCDHW'), precision=lax.Precision.HIGHEST)[0]

def weight_conv(operand, upstream):
    result = lax.conv_general_dilated(operand[None].astype(jnp.float32), upstream[None].astype(jnp.float32), (1, 1, 1), 'VALID', dimension_numbers=('CNDHW', 'IODHW', 'NCDHW'), precision=lax.Precision.HIGHEST)
    return jnp.transpose(result, (1, 0, 2, 3, 4))

def reference(field, cotangent, cosmology, lift_weight, lift_bias, style_weight, style_bias, kernel, offset):
    lifted, hidden, styles, modded, inv_norm, scaled = modulate(cosmology, lift_weight, lift_bias, style_weight, style_bias, kernel)
    flipped = jnp.transpose(scaled[:, :, ::-1, ::-1, ::-1], (1, 0, 2, 3, 4))
    padded = jnp.pad(field, ((0, 0), (1, 1), (1, 1), (1, 1)), mode='wrap')
    slab_count = NX // CX

    def forward_slab(slab_index):
        first_plane = (slab_index * CX).astype(jnp.int32)
        slab_block = lax.dynamic_slice_in_dim(padded, first_plane, CX + 2, 1)
        preact = conv_valid(slab_block, scaled) + offset[:, None, None, None]
        slab_cotan = lax.dynamic_slice_in_dim(cotangent, first_plane, CX, 1)
        upstream = (slab_cotan.astype(jnp.float32) * silu_slope(preact)).astype(jnp.bfloat16)
        part_kernel = weight_conv(slab_block, upstream)
        part_offset = lax.optimization_barrier(jnp.sum(upstream.astype(jnp.float32), axis=(1, 2, 3)))
        return (upstream, part_kernel, part_offset)
    upstreams, kernel_parts, offset_parts = lax.map(forward_slab, jnp.arange(slab_count, dtype=jnp.int32))
    upstream_all = jnp.moveaxis(upstreams, 0, 1).reshape(C, NX, NY, NZ)
    grad_pad = jnp.pad(upstream_all, ((0, 0), (1, 1), (1, 1), (1, 1)), mode='wrap')

    def input_slab(slab_index):
        first_plane = (slab_index * CX).astype(jnp.int32)
        slab_block = lax.dynamic_slice_in_dim(grad_pad, first_plane, CX + 2, 1)
        return conv_valid(slab_block, flipped).astype(jnp.bfloat16)
    grad_slabs = lax.map(input_slab, jnp.arange(slab_count, dtype=jnp.int32))
    grad_field = jnp.moveaxis(grad_slabs, 0, 1).reshape(C, NX, NY, NZ)
    sums_kernel = lax.optimization_barrier(jnp.sum(kernel_parts, axis=0))
    sums_offset = lax.optimization_barrier(jnp.sum(offset_parts, axis=0))
    grad_kernel, grad_offset, grad_lift, grad_liftbias, grad_style, grad_stylebias = param_backward(sums_kernel, sums_offset, cosmology, style_weight, kernel, lifted, hidden, styles, modded, inv_norm)
    return (grad_field, grad_kernel, grad_offset, grad_lift, grad_liftbias, grad_style, grad_stylebias)
```

```python
import functools

import jax
import jax.numpy as jnp
from jax import lax
from jax.experimental import pallas as pl
from jax.experimental.pallas import tpu as pltpu
from jax.sharding import PartitionSpec as P

demod_eps = 1e-06
clip_eps = 1e-06
MESH = pl.DeviceIdType.MESH
SIDES = tuple((dx, dy) for dx in (-1, 0, 1) for dy in (-1, 0, 1) if (dx, dy) != (0, 0))


def silu_slope(values):
    logistic = 1.0 / (1.0 + jnp.exp(-values))
    return logistic * (1.0 + values * (1.0 - logistic))


def kernel_body(
    sizes,
    field, cotangent, cosmology, lift_weight, lift_bias, style_t, style_bias, kernel, offset,
    grad, grad_kernel, grad_offset, grad_lift, grad_liftbias, grad_style_t, grad_stylebias,
    field_ext, up_ext, field_taps, up_taps, edge_out, edge_in, w_fwd, w_bwd, packed,
    share, from_z, part_z, from_y, part_y, from_x, total,
    xy_send, xy_recv, z_send, z_recv, rz_send, rz_recv, ry_send, ry_recv, rx_send, rx_recv,
    gy_send, gy_recv, gz_send, gz_recv,
):
    nx, ny, nz = sizes
    C, CX, CY, CZ = field.shape[2], field.shape[0], field.shape[1], field.shape[3]
    EY = CY + 2
    taps = kernel.shape[0]
    per = CZ // C
    tiles = (taps + per) // per
    me_x, me_y, me_z = (lax.axis_index("gx"), lax.axis_index("gy"), lax.axis_index("gz"))

    def at(dx=0, dy=0, dz=0):
        return (
            lax.rem(me_x + (dx + nx), nx) if dx else me_x,
            lax.rem(me_y + (dy + ny), ny) if dy else me_y,
            lax.rem(me_z + (dz + nz), nz) if dz else me_z,
        )

    partners = [at(dx, dy) for dx, dy in SIDES]
    partners += [at(dz=k) for k in range(1, nz)]
    partners += [at(dy=k) for k in range(1, ny)]
    partners += [at(dx=k) for k in range(1, nx)]
    barrier = pltpu.get_barrier_semaphore()
    for partner in partners:
        pl.semaphore_signal(barrier, inc=1, device_id=partner, device_id_type=MESH)

    def remote(src, dst, send, recv, device):
        return pltpu.make_async_remote_copy(
            src_ref=src, dst_ref=dst, send_sem=send, recv_sem=recv, device_id=device,
            device_id_type=MESH,
        )

    def span(step, count, first):
        if step == 0:
            return pl.ds(first, count), pl.ds(1, count)
        if step > 0:
            return pl.ds(first + count - 1, 1), pl.ds(0, 1)
        return pl.ds(first, 1), pl.ds(count + 1, 1)

    def side_copies(which, source, first, ext):
        copies = []
        for at_side, (dx, dy) in enumerate(SIDES):
            sx, tx = span(dx, CX, first)
            sy, ty = span(dy, CY, first)
            copies.append(
                remote(source.at[sx, sy], ext.at[tx, ty], xy_send.at[which, at_side],
                       xy_recv.at[which, at_side], at(dx, dy))
            )
        return copies

    lanes = lax.broadcasted_iota(jnp.int32, (C, CZ), 1)
    group = lax.div(lanes, 2)

    def edge_copies(which):
        return [
            remote(edge_out.at[which], edge_in.at[which, 0], z_send.at[which, 0],
                   z_recv.at[which, 0], at(dz=1)),
            remote(edge_out.at[which], edge_in.at[which, 1], z_send.at[which, 1],
                   z_recv.at[which, 1], at(dz=-1)),
        ]

    def pack_edges(which, ext):
        def plane(p, edges):
            for y in range(EY):
                row = p * EY + y
                rolled = pltpu.roll(ext[p, y].astype(jnp.float32), 1 + 2 * row, 1)
                edges = jnp.where(group == row, rolled, edges)
            return edges

        edges = lax.fori_loop(0, CX + 2, plane, jnp.zeros((C, CZ), jnp.float32))
        edge_out[which] = edges.astype(jnp.bfloat16)

    def build_taps(which, ext, out):
        before = edge_in[which, 0].astype(jnp.float32)
        after = edge_in[which, 1].astype(jnp.float32)

        def plane(p, carry):
            for y in range(EY):
                row = p * EY + y
                mid = ext[p, y]
                wide = mid.astype(jnp.float32)
                low = jnp.where(lanes == 0, pltpu.roll(before, lax.rem(CZ - 2 * row, CZ), 1),
                                pltpu.roll(wide, 1, 1))
                high = jnp.where(lanes == CZ - 1, pltpu.roll(after, CZ - 2 - 2 * row, 1),
                                 pltpu.roll(wide, CZ - 1, 1))
                out[p, y, 0:C] = low.astype(jnp.bfloat16)
                out[p, y, C : 2 * C] = mid
                out[p, y, 2 * C : 3 * C] = high.astype(jnp.bfloat16)
            return carry

        lax.fori_loop(0, CX + 2, plane, 0)

    def columns(source, x, y):
        both = []
        for k in range(2):
            planes = [source[x + a, pl.ds(y + k, 3)].reshape(9 * C, CZ) for a in range(3)]
            both.append(jnp.concatenate(planes, axis=0))
        return jnp.concatenate(both, axis=1)

    field_ext[1 : CX + 1, 1 : CY + 1] = field[...]
    pl.semaphore_wait(barrier, len(partners))
    field_sides = side_copies(0, field, 0, field_ext)
    for copy in field_sides:
        copy.start()

    eye = lax.broadcasted_iota(jnp.int32, (C, C), 0) == lax.broadcasted_iota(jnp.int32, (C, C), 1)

    def to_row(column):
        return jnp.sum(jnp.where(eye, column, 0.0), axis=0, keepdims=True)

    def to_column(row):
        return jnp.sum(jnp.where(eye, row, 0.0), axis=1, keepdims=True)

    lifted = lift_bias[...]
    for k in range(lift_weight.shape[0]):
        lifted = lifted + cosmology[0:1, k : k + 1] * lift_weight[k : k + 1, :]
    hidden = lifted / (1.0 + jnp.exp(-lifted))
    styles_column = (
        jnp.sum(style_t[...] * hidden, axis=1, keepdims=True) + to_column(style_bias[...]) + 1.0
    )
    styles = to_row(styles_column)
    styles_wide = jnp.concatenate([styles] * per, axis=1)
    squares = jnp.zeros((C, CZ), jnp.float32)
    for j in range(tiles):
        members = [
            kernel[per * j + k] if per * j + k < taps else jnp.zeros((C, C), jnp.float32)
            for k in range(per)
        ]
        tile = jnp.concatenate(members, axis=1)
        packed[j] = tile
        modded = tile * styles_wide
        squares = squares + modded * modded
    inv_norm = lax.rsqrt(jnp.sum(squares, axis=1, keepdims=True) + demod_eps)
    turned = []
    for j in range(tiles):
        scaled = packed[j] * styles_wide * inv_norm
        w_fwd[:, j * CZ : (j + 1) * CZ] = scaled.astype(jnp.bfloat16)
        flat = scaled.T
        turned += [flat[k * C : (k + 1) * C] for k in range(per)]
    turned = turned[:taps][::-1] + [jnp.zeros((C, C), jnp.float32)] * (tiles * per - taps)
    for j in range(tiles):
        w_bwd[:, j * CZ : (j + 1) * CZ] = jnp.concatenate(
            turned[per * j : per * (j + 1)], axis=1
        ).astype(jnp.bfloat16)
    offset_column = to_column(offset[...])

    for copy in field_sides:
        copy.wait()
    pack_edges(0, field_ext)
    field_edges = edge_copies(0)
    for copy in field_edges:
        copy.start()
    for copy in field_edges:
        copy.wait()
    build_taps(0, field_ext, field_taps)

    depth = taps * C

    def forward(x, carry):
        for y in range(0, CY, 2):
            preact = jnp.dot(w_fwd[:, :depth], columns(field_taps, x, y),
                             preferred_element_type=jnp.float32) + offset_column
            cot = jnp.concatenate([cotangent[x, y], cotangent[x, y + 1]], axis=1)
            upstream = (cot.astype(jnp.float32) * silu_slope(preact)).astype(jnp.bfloat16)
            up_ext[x + 1, y + 1] = upstream[:, :CZ]
            up_ext[x + 1, y + 2] = upstream[:, CZ:]
        return carry

    lax.fori_loop(0, CX, forward, 0)
    up_sides = side_copies(1, up_ext, 1, up_ext)
    for copy in up_sides:
        copy.start()

    def weigh(x, carry):
        sums, offsets = carry
        for y in range(0, CY, 2):
            upstream = jnp.concatenate([up_ext[x + 1, y + 1], up_ext[x + 1, y + 2]], axis=1)
            sums = sums + lax.dot_general(
                upstream, columns(field_taps, x, y), (((1,), (1,)), ((), ())),
                preferred_element_type=jnp.float32,
            )
            wide = upstream.astype(jnp.float32)
            offsets = offsets + wide[:, :CZ] + wide[:, CZ:]
        return (sums, offsets)

    sums, offsets = lax.fori_loop(
        0, CX, weigh,
        (jnp.zeros((C, depth), jnp.float32), jnp.zeros((C, CZ), jnp.float32)),
    )
    offset_sum = jnp.sum(offsets, axis=1, keepdims=True)
    rows = C * tiles
    share[...] = jnp.zeros_like(share)
    for j in range(tiles):
        if (j + 1) * CZ <= depth:
            share[j * C : (j + 1) * C] = sums[:, j * CZ : (j + 1) * CZ]
        else:
            used = depth - j * CZ
            share[j * C : (j + 1) * C] = jnp.concatenate(
                [sums[:, j * CZ : depth], jnp.broadcast_to(offset_sum, (C, CZ - used))], axis=1
            )

    rows_z = share.shape[0] // nz
    rows_y = rows_z // ny

    def rows_at(base, count):
        return pl.ds(pl.multiple_of(base, 8), count)

    reduce_z = []
    for k in range(1, nz):
        there = at(dz=k)
        reduce_z.append(remote(share.at[rows_at(there[2] * rows_z, rows_z)], from_z.at[k - 1],
                               rz_send.at[k - 1], rz_recv.at[k - 1], there))
    for copy in reduce_z:
        copy.start()

    for copy in up_sides:
        copy.wait()
    pack_edges(1, up_ext)
    up_edges = edge_copies(1)
    for copy in up_edges:
        copy.start()

    for copy in reduce_z:
        copy.wait()
    mine = share[rows_at(me_z * rows_z, rows_z), :]
    for k in range(1, nz):
        mine = mine + from_z[k - 1]
    part_z[...] = mine
    reduce_y = []
    for k in range(1, ny):
        there = at(dy=k)
        reduce_y.append(remote(part_z.at[rows_at(there[1] * rows_y, rows_y)], from_y.at[k - 1],
                               ry_send.at[k - 1], ry_recv.at[k - 1], there))
    for copy in reduce_y:
        copy.start()

    for copy in up_edges:
        copy.wait()
    build_taps(1, up_ext, up_taps)

    for copy in reduce_y:
        copy.wait()
    mine = part_z[rows_at(me_y * rows_y, rows_y), :]
    for k in range(1, ny):
        mine = mine + from_y[k - 1]
    part_y[...] = mine
    from_x[me_x] = mine
    reduce_x = [
        remote(part_y, from_x.at[me_x], rx_send.at[k - 1], rx_recv.at[k - 1], at(dx=k))
        for k in range(1, nx)
    ]
    for copy in reduce_x:
        copy.start()

    def backward(x, carry):
        for y in range(0, CY, 2):
            result = jnp.dot(w_bwd[:, :depth], columns(up_taps, x, y),
                             preferred_element_type=jnp.float32).astype(jnp.bfloat16)
            grad[x, y] = result[:, :CZ]
            grad[x, y + 1] = result[:, CZ:]
        return carry

    lax.fori_loop(0, 1, backward, 0)

    for copy in reduce_x:
        copy.wait()
    mine = from_x[0]
    for k in range(1, nx):
        mine = mine + from_x[k]
    own_y = rows_at(me_z * rows_z + me_y * rows_y, rows_y)
    total[own_y, :] = mine
    gather_y = [
        remote(total.at[own_y], total.at[own_y], gy_send.at[k - 1], gy_recv.at[k - 1], at(dy=k))
        for k in range(1, ny)
    ]
    for copy in gather_y:
        copy.start()
    lax.fori_loop(1, 2, backward, 0)
    for copy in gather_y:
        copy.wait()
    own_z = rows_at(me_z * rows_z, rows_z)
    gather_z = [
        remote(total.at[own_z], total.at[own_z], gz_send.at[k - 1], gz_recv.at[k - 1], at(dz=k))
        for k in range(1, nz)
    ]
    for copy in gather_z:
        copy.start()
    lax.fori_loop(2, CX, backward, 0)
    for copy in gather_z:
        copy.wait()

    last = taps - per * (tiles - 1)
    projected = jnp.zeros((C, CZ), jnp.float32)
    sum_tiles, modded_tiles = [], []
    for j in range(tiles):
        tile = total[j * C : (j + 1) * C, :]
        if j == tiles - 1:
            offset_row = to_row(tile[:, last * C : last * C + 1])
            tile = jnp.where(lanes < last * C, tile, 0.0)
        modded = packed[j] * styles_wide
        projected = projected + tile * modded
        sum_tiles.append(tile)
        modded_tiles.append(modded)
    projected = jnp.sum(projected, axis=1, keepdims=True)
    scale = inv_norm * inv_norm * projected
    raws = []
    square = jnp.zeros((C, CZ), jnp.float32)
    along = jnp.zeros((C, CZ), jnp.float32)
    for j in range(tiles):
        mod_grad = inv_norm * (sum_tiles[j] - modded_tiles[j] * scale)
        raw = mod_grad * styles_wide
        along = along + mod_grad * packed[j]
        square = square + raw * raw
        raws.append(raw)
    along = jnp.sum(along, axis=0, keepdims=True)
    styles_grad = along[:, 0:C]
    for k in range(1, per):
        styles_grad = styles_grad + along[:, k * C : (k + 1) * C]
    styles_grad_column = to_column(styles_grad)
    hidden_grad = jnp.sum(style_t[...] * styles_grad_column, axis=0, keepdims=True)
    lifted_grad = hidden_grad * silu_slope(lifted)
    style_raw = styles_grad_column * hidden
    lift_raws = [
        cosmology[0:1, k : k + 1] * lifted_grad for k in range(lift_weight.shape[0])
    ]

    def sum_all(values):
        return jnp.sum(jnp.sum(values, axis=1, keepdims=True), axis=0, keepdims=True)

    square_sum = sum_all(square)
    for member in [offset_row, lifted_grad, style_raw, styles_grad] + lift_raws:
        square_sum = square_sum + sum_all(member * member)
    entries = taps * C * C + 2 * C + (1 + lift_weight.shape[0] + C) * lifted.shape[1]
    factor = jnp.minimum(1.0, lax.rsqrt(square_sum / entries + clip_eps))
    for j in range(tiles):
        scaled_raw = raws[j] * factor
        for k in range(per):
            if per * j + k < taps:
                grad_kernel[per * j + k] = scaled_raw[:, k * C : (k + 1) * C]
    grad_offset[...] = offset_row * factor
    for k in range(lift_weight.shape[0]):
        grad_lift[k : k + 1, :] = lift_raws[k] * factor
    grad_liftbias[...] = lifted_grad * factor
    grad_style_t[...] = style_raw * factor
    grad_stylebias[...] = styles_grad * factor


def body(
    sizes, field, cotangent, cosmology, lift_weight, lift_bias, style_weight, style_bias, kernel,
    offset,
):
    nx, ny, nz = sizes
    C, CX, CY, CZ = field.shape
    HID = lift_bias.shape[0]
    taps = kernel.shape[2] * kernel.shape[3] * kernel.shape[4]
    per = CZ // C
    tiles = (taps + per) // per
    unit = nz * ny * 8
    rows = -(-tiles * C // unit) * unit
    f32, bf16 = jnp.float32, jnp.bfloat16
    dma = pltpu.SemaphoreType.DMA
    vmem = pl.BlockSpec(memory_space=pltpu.VMEM)
    results = pl.pallas_call(
        functools.partial(kernel_body, sizes),
        out_shape=[
            jax.ShapeDtypeStruct((CX, CY, C, CZ), bf16),
            jax.ShapeDtypeStruct((taps, C, C), f32),
            jax.ShapeDtypeStruct((1, C), f32),
            jax.ShapeDtypeStruct(lift_weight.shape, f32),
            jax.ShapeDtypeStruct((1, HID), f32),
            jax.ShapeDtypeStruct((C, HID), f32),
            jax.ShapeDtypeStruct((1, C), f32),
        ],
        in_specs=[vmem] * 9,
        out_specs=[vmem] * 7,
        scratch_shapes=[
            pltpu.VMEM((CX + 2, CY + 2, C, CZ), bf16),
            pltpu.VMEM((CX + 2, CY + 2, C, CZ), bf16),
            pltpu.VMEM((CX + 2, CY + 2, 3 * C, CZ), bf16),
            pltpu.VMEM((CX + 2, CY + 2, 3 * C, CZ), bf16),
            pltpu.VMEM((2, C, CZ), bf16),
            pltpu.VMEM((2, 2, C, CZ), bf16),
            pltpu.VMEM((C, tiles * CZ), bf16),
            pltpu.VMEM((C, tiles * CZ), bf16),
            pltpu.VMEM((tiles, C, CZ), f32),
            pltpu.VMEM((rows, CZ), f32),
            pltpu.VMEM((nz - 1, rows // nz, CZ), f32),
            pltpu.VMEM((rows // nz, CZ), f32),
            pltpu.VMEM((ny - 1, rows // nz // ny, CZ), f32),
            pltpu.VMEM((rows // nz // ny, CZ), f32),
            pltpu.VMEM((nx, rows // nz // ny, CZ), f32),
            pltpu.VMEM((rows, CZ), f32),
            dma((2, 8)), dma((2, 8)), dma((2, 2)), dma((2, 2)),
            dma((nz - 1,)), dma((nz - 1,)), dma((ny - 1,)), dma((ny - 1,)),
            dma((nx - 1,)), dma((nx - 1,)), dma((ny - 1,)), dma((ny - 1,)),
            dma((nz - 1,)), dma((nz - 1,)),
        ],
        compiler_params=pltpu.CompilerParams(
            collective_id=0, has_side_effects=True, vmem_limit_bytes=32 * 1024 * 1024
        ),
    )(
        jnp.transpose(field, (1, 2, 0, 3)),
        jnp.transpose(cotangent, (1, 2, 0, 3)),
        cosmology[None],
        lift_weight,
        lift_bias[None],
        style_weight.T,
        style_bias[None],
        jnp.transpose(kernel, (2, 3, 4, 0, 1)).reshape(taps, C, C),
        offset[None],
    )
    grad, grad_kernel, grad_offset, grad_lift, grad_liftbias, grad_style_t, grad_stylebias = results
    return (
        jnp.transpose(grad, (2, 0, 1, 3)),
        jnp.transpose(grad_kernel.reshape(kernel.shape[2:] + (C, C)), (3, 4, 0, 1, 2)),
        grad_offset[0],
        grad_lift,
        grad_liftbias[0],
        grad_style_t.T,
        grad_stylebias[0],
    )


def solution(mesh):
    sizes = (mesh.shape["gx"], mesh.shape["gy"], mesh.shape["gz"])
    placed = P(None, "gx", "gy", "gz")
    return jax.shard_map(
        functools.partial(body, sizes),
        mesh=mesh,
        in_specs=(placed, placed, P(), P(), P(), P(), P(), P(), P()),
        out_specs=(placed, P(), P(), P(), P(), P(), P()),
        check_vma=False,
    )
```

```python
import functools

import jax
import jax.numpy as jnp
from jax import lax
from jax.experimental import pallas as pl
from jax.experimental.pallas import tpu as pltpu
from jax.sharding import PartitionSpec as P

demod_eps = 1e-06
clip_eps = 1e-06
MESH = pl.DeviceIdType.MESH
SIDES = tuple((dx, dy) for dx in (-1, 0, 1) for dy in (-1, 0, 1) if (dx, dy) != (0, 0))


def silu_slope(values):
    logistic = 1.0 / (1.0 + jnp.exp(-values))
    return logistic * (1.0 + values * (1.0 - logistic))


def kernel_body(
    sizes,
    field, cotangent, cosmology, lift_weight, lift_bias, style_t, style_bias, kernel, offset,
    grad, grad_packed, grad_rows, grad_style_t,
    field_ext, up_ext, field_taps, up_taps, edge_out, edge_in, w_fwd, w_bwd, packed, cot, turned_back,
    share, from_z, part_z, from_xy, total,
    xy_send, xy_recv, z_send, z_recv, rz_send, rz_recv, rxy_send, rxy_recv, g_send, g_recv,
):
    nx, ny, nz = sizes
    C, CX, CY, CZ = field.shape
    EY = CY + 2
    taps = kernel.shape[0]
    per = CZ // C
    tiles = (taps + per) // per
    me_x, me_y, me_z = (lax.axis_index("gx"), lax.axis_index("gy"), lax.axis_index("gz"))

    def at(dx=0, dy=0, dz=0):
        return (
            lax.rem(me_x + (dx + nx), nx) if dx else me_x,
            lax.rem(me_y + (dy + ny), ny) if dy else me_y,
            lax.rem(me_z + (dz + nz), nz) if dz else me_z,
        )

    partners = [at(dx, dy) for dx, dy in SIDES]
    plane_xy = [(dx, dy) for dx in range(nx) for dy in range(ny) if (dx, dy) != (0, 0)]
    plane_yz = [(dy, dz) for dy in range(ny) for dz in range(nz) if (dy, dz) != (0, 0)]
    partners += [at(dx, dy) for dx, dy in plane_xy]
    partners += [at(0, dy, dz) for dy, dz in plane_yz]
    barrier = pltpu.get_barrier_semaphore()
    for partner in partners:
        pl.semaphore_signal(barrier, inc=1, device_id=partner, device_id_type=MESH)

    def remote(src, dst, send, recv, device):
        return pltpu.make_async_remote_copy(
            src_ref=src, dst_ref=dst, send_sem=send, recv_sem=recv, device_id=device,
            device_id_type=MESH,
        )

    def span(step, count, first):
        if step == 0:
            return pl.ds(first, count), pl.ds(1, count)
        if step > 0:
            return pl.ds(first + count - 1, 1), pl.ds(0, 1)
        return pl.ds(first, 1), pl.ds(count + 1, 1)

    def side_copies(which, source, first, ext):
        copies = []
        for at_side, (dx, dy) in enumerate(SIDES):
            sx, tx = span(dx, CX, first)
            sy, ty = span(dy, CY, first)
            copies.append(
                remote(source.at[sx, sy], ext.at[tx, ty], xy_send.at[which, at_side],
                       xy_recv.at[which, at_side], at(dx, dy))
            )
        return copies

    lanes = lax.broadcasted_iota(jnp.int32, (C, CZ), 1)
    group = lax.div(lanes, 2)

    def edge_copies(which):
        return [
            remote(edge_out.at[which], edge_in.at[which, 0], z_send.at[which, 0],
                   z_recv.at[which, 0], at(dz=1)),
            remote(edge_out.at[which], edge_in.at[which, 1], z_send.at[which, 1],
                   z_recv.at[which, 1], at(dz=-1)),
        ]

    def pack_edges(which, ext):
        def plane(p, edges):
            for y in range(EY):
                row = p * EY + y
                rolled = pltpu.roll(ext[p, y].astype(jnp.float32), 1 + 2 * row, 1)
                edges = jnp.where(group == row, rolled, edges)
            return edges

        edges = lax.fori_loop(0, CX + 2, plane, jnp.zeros((C, CZ), jnp.float32))
        edge_out[which] = edges.astype(jnp.bfloat16)

    def build_taps(which, ext, out):
        before = edge_in[which, 0].astype(jnp.float32)
        after = edge_in[which, 1].astype(jnp.float32)

        def plane(p, carry):
            for y in range(EY):
                row = p * EY + y
                mid = ext[p, y]
                wide = mid.astype(jnp.float32)
                low = jnp.where(lanes == 0, pltpu.roll(before, lax.rem(CZ - 2 * row, CZ), 1),
                                pltpu.roll(wide, 1, 1))
                high = jnp.where(lanes == CZ - 1, pltpu.roll(after, CZ - 2 - 2 * row, 1),
                                 pltpu.roll(wide, CZ - 1, 1))
                out[p, y, 0:C] = low.astype(jnp.bfloat16)
                out[p, y, C : 2 * C] = mid
                out[p, y, 2 * C : 3 * C] = high.astype(jnp.bfloat16)
            return carry

        lax.fori_loop(0, CX + 2, plane, 0)

    def columns(source, x, y):
        both = []
        for k in range(2):
            planes = [source[x + a, pl.ds(y + k, 3)].reshape(9 * C, CZ) for a in range(3)]
            both.append(jnp.concatenate(planes, axis=0))
        return jnp.concatenate(both, axis=1)

    for x in range(CX):
        turned_x = jnp.swapaxes(field[:, x].astype(jnp.float32), 0, 1)
        field_ext[x + 1, 1 : CY + 1] = turned_x.astype(jnp.bfloat16)
    pl.semaphore_wait(barrier, len(partners))
    field_sides = side_copies(0, field_ext, 1, field_ext)
    for copy in field_sides:
        copy.start()

    eye = lax.broadcasted_iota(jnp.int32, (C, C), 0) == lax.broadcasted_iota(jnp.int32, (C, C), 1)

    def to_row(column):
        return jnp.sum(jnp.where(eye, column, 0.0), axis=0, keepdims=True)

    def to_column(row):
        return jnp.sum(jnp.where(eye, row, 0.0), axis=1, keepdims=True)

    lifted = lift_bias[...]
    for k in range(lift_weight.shape[0]):
        lifted = lifted + cosmology[0:1, k : k + 1] * lift_weight[k : k + 1, :]
    hidden = lifted / (1.0 + jnp.exp(-lifted))
    styles_column = (
        jnp.sum(style_t[...] * hidden, axis=1, keepdims=True) + to_column(style_bias[...]) + 1.0
    )
    styles = to_row(styles_column)
    styles_wide = jnp.concatenate([styles] * per, axis=1)
    squares = jnp.zeros((C, CZ), jnp.float32)
    for j in range(tiles):
        members = [
            kernel[per * j + k] if per * j + k < taps else jnp.zeros((C, C), jnp.float32)
            for k in range(per)
        ]
        tile = jnp.concatenate(members, axis=1)
        packed[j] = tile
        modded = tile * styles_wide
        squares = squares + modded * modded
    inv_norm = lax.rsqrt(jnp.sum(squares, axis=1, keepdims=True) + demod_eps)
    turned = []
    for j in range(tiles):
        scaled = packed[j] * styles_wide * inv_norm
        w_fwd[:, j * CZ : (j + 1) * CZ] = scaled.astype(jnp.bfloat16)
        flat = scaled.T
        turned += [flat[k * C : (k + 1) * C] for k in range(per)]
    turned = turned[:taps][::-1] + [jnp.zeros((C, C), jnp.float32)] * (tiles * per - taps)
    for j in range(tiles):
        w_bwd[:, j * CZ : (j + 1) * CZ] = jnp.concatenate(
            turned[per * j : per * (j + 1)], axis=1
        ).astype(jnp.bfloat16)
    offset_column = to_column(offset[...])
    for x in range(CX):
        cot[x] = jnp.swapaxes(cotangent[:, x].astype(jnp.float32), 0, 1)

    for copy in field_sides:
        copy.wait()
    pack_edges(0, field_ext)
    field_edges = edge_copies(0)
    for copy in field_edges:
        copy.start()
    for copy in field_edges:
        copy.wait()
    build_taps(0, field_ext, field_taps)

    depth = taps * C

    def forward(x, carry):
        for y in range(0, CY, 2):
            preact = jnp.dot(w_fwd[:, :depth], columns(field_taps, x, y),
                             preferred_element_type=jnp.float32) + offset_column
            above = jnp.concatenate([cot[x, y], cot[x, y + 1]], axis=1)
            upstream = (above * silu_slope(preact)).astype(jnp.bfloat16)
            up_ext[x + 1, y + 1] = upstream[:, :CZ]
            up_ext[x + 1, y + 2] = upstream[:, CZ:]
        return carry

    lax.fori_loop(0, CX, forward, 0)
    up_sides = side_copies(1, up_ext, 1, up_ext)
    for copy in up_sides:
        copy.start()

    def weigh(x, carry):
        sums, offsets = carry
        for y in range(0, CY, 2):
            upstream = jnp.concatenate([up_ext[x + 1, y + 1], up_ext[x + 1, y + 2]], axis=1)
            sums = sums + lax.dot_general(
                upstream, columns(field_taps, x, y), (((1,), (1,)), ((), ())),
                preferred_element_type=jnp.float32,
            )
            wide = upstream.astype(jnp.float32)
            offsets = offsets + wide[:, :CZ] + wide[:, CZ:]
        return (sums, offsets)

    sums, offsets = lax.fori_loop(
        0, CX, weigh,
        (jnp.zeros((C, depth), jnp.float32), jnp.zeros((C, CZ), jnp.float32)),
    )
    offset_sum = jnp.sum(offsets, axis=1, keepdims=True)
    for j in range(share.shape[0] // C):
        if (j + 1) * CZ <= depth:
            tile = sums[:, j * CZ : (j + 1) * CZ]
        elif j < tiles:
            used = depth - j * CZ
            tile = jnp.concatenate(
                [sums[:, j * CZ : depth], jnp.broadcast_to(offset_sum, (C, CZ - used))], axis=1
            )
        else:
            tile = jnp.zeros((C, CZ), jnp.float32)
        share[j * C : (j + 1) * C] = tile.astype(jnp.bfloat16)

    rows_z = share.shape[0] // nz
    rows_y = rows_z // ny

    def rows_at(base, count):
        return pl.ds(pl.multiple_of(base, 16), count)

    reduce_z = []
    for k in range(1, nz):
        there = at(dz=k)
        reduce_z.append(remote(share.at[rows_at(there[2] * rows_z, rows_z)], from_z.at[k - 1],
                               rz_send.at[k - 1], rz_recv.at[k - 1], there))
    for copy in reduce_z:
        copy.start()

    for copy in up_sides:
        copy.wait()
    pack_edges(1, up_ext)
    up_edges = edge_copies(1)
    for copy in up_edges:
        copy.start()

    for copy in reduce_z:
        copy.wait()
    mine = share[rows_at(me_z * rows_z, rows_z), :].astype(jnp.float32)
    for k in range(1, nz):
        mine = mine + from_z[k - 1].astype(jnp.float32)
    part_z[...] = mine.astype(jnp.bfloat16)
    my_slot = me_x * ny + me_y
    reduce_xy = []
    for k, (dx, dy) in enumerate(plane_xy):
        there = at(dx, dy)
        reduce_xy.append(remote(part_z.at[rows_at(there[1] * rows_y, rows_y)], from_xy.at[my_slot],
                                rxy_send.at[k], rxy_recv.at[k], there))
    for copy in reduce_xy:
        copy.start()
    from_xy[my_slot] = part_z[rows_at(me_y * rows_y, rows_y), :]

    for copy in up_edges:
        copy.wait()
    build_taps(1, up_ext, up_taps)

    def backward(x, carry):
        for y in range(0, CY, 2):
            result = jnp.dot(w_bwd[:, :depth], columns(up_taps, x, y),
                             preferred_element_type=jnp.float32)
            turned_back[y] = result[:, :CZ]
            turned_back[y + 1] = result[:, CZ:]
        grad[:, x] = jnp.swapaxes(turned_back[...], 0, 1).astype(jnp.bfloat16)
        return carry

    lax.fori_loop(0, 1, backward, 0)

    for copy in reduce_xy:
        copy.wait()
    mine = from_xy[0].astype(jnp.float32)
    for k in range(1, nx * ny):
        mine = mine + from_xy[k].astype(jnp.float32)
    own = rows_at(me_z * rows_z + me_y * rows_y, rows_y)
    total[own, :] = mine.astype(jnp.bfloat16)
    gather = [
        remote(total.at[own], total.at[own], g_send.at[k], g_recv.at[k], at(0, dy, dz))
        for k, (dy, dz) in enumerate(plane_yz)
    ]
    for copy in gather:
        copy.start()
    lax.fori_loop(1, CX, backward, 0)
    for copy in gather:
        copy.wait()

    last = taps - per * (tiles - 1)
    projected = jnp.zeros((C, CZ), jnp.float32)
    sum_tiles, modded_tiles = [], []
    for j in range(tiles):
        tile = total[j * C : (j + 1) * C, :].astype(jnp.float32)
        if j == tiles - 1:
            offset_row = to_row(tile[:, last * C : last * C + 1])
            tile = jnp.where(lanes < last * C, tile, 0.0)
        modded = packed[j] * styles_wide
        projected = projected + tile * modded
        sum_tiles.append(tile)
        modded_tiles.append(modded)
    projected = jnp.sum(projected, axis=1, keepdims=True)
    scale = inv_norm * inv_norm * projected
    raws = []
    square = jnp.zeros((C, CZ), jnp.float32)
    along = jnp.zeros((C, CZ), jnp.float32)
    for j in range(tiles):
        mod_grad = inv_norm * (sum_tiles[j] - modded_tiles[j] * scale)
        raw = mod_grad * styles_wide
        along = along + mod_grad * packed[j]
        square = square + raw * raw
        raws.append(raw)
    along = jnp.sum(along, axis=0, keepdims=True)
    styles_grad = along[:, 0:C]
    for k in range(1, per):
        styles_grad = styles_grad + along[:, k * C : (k + 1) * C]
    styles_grad_column = to_column(styles_grad)
    hidden_grad = jnp.sum(style_t[...] * styles_grad_column, axis=0, keepdims=True)
    lifted_grad = hidden_grad * silu_slope(lifted)
    style_raw = styles_grad_column * hidden
    lift_raws = [
        cosmology[0:1, k : k + 1] * lifted_grad for k in range(lift_weight.shape[0])
    ]

    def sum_all(values):
        return jnp.sum(jnp.sum(values, axis=1, keepdims=True), axis=0, keepdims=True)

    square_sum = sum_all(square)
    for member in [offset_row, lifted_grad, style_raw, styles_grad] + lift_raws:
        square_sum = square_sum + sum_all(member * member)
    entries = taps * C * C + 2 * C + (1 + lift_weight.shape[0] + C) * lifted.shape[1]
    factor = jnp.minimum(1.0, lax.rsqrt(square_sum / entries + clip_eps))
    for j in range(tiles):
        grad_packed[j] = raws[j] * factor
    grad_style_t[...] = style_raw * factor
    wide = lifted.shape[1]
    small = jnp.concatenate([offset_row, styles_grad], axis=1)
    grad_rows[0:1, 0 : 2 * C] = small * factor
    grad_rows[1:2, :] = lifted_grad * factor
    for k in range(lift_weight.shape[0]):
        grad_rows[k + 2 : k + 3, :] = lift_raws[k] * factor


def hand_out(
    grad_in, grad_packed, grad_rows, grad_style_in,
    grad, grad_kernel, grad_offset, grad_lift, grad_liftbias, grad_style_t, grad_stylebias,
):
    C = grad_packed.shape[1]
    per = grad_packed.shape[2] // C
    grad[...] = grad_in[...]
    for t in range(grad_kernel.shape[0]):
        k = t % per
        grad_kernel[t] = grad_packed[t // per][:, k * C : (k + 1) * C]
    grad_offset[...] = grad_rows[0:1, 0:C]
    grad_stylebias[...] = grad_rows[0:1, C : 2 * C]
    grad_liftbias[...] = grad_rows[1:2, :]
    grad_lift[...] = grad_rows[2 : 2 + grad_lift.shape[0], :]
    grad_style_t[...] = grad_style_in[...]


def body(
    sizes, field, cotangent, cosmology, lift_weight, lift_bias, style_weight, style_bias, kernel,
    offset,
):
    nx, ny, nz = sizes
    C, CX, CY, CZ = field.shape
    HID = lift_bias.shape[0]
    taps = kernel.shape[2] * kernel.shape[3] * kernel.shape[4]
    per = CZ // C
    tiles = (taps + per) // per
    unit = nz * ny * 16
    rows = -(-tiles * C // unit) * unit
    f32, bf16 = jnp.float32, jnp.bfloat16
    dma = pltpu.SemaphoreType.DMA
    vmem = pl.BlockSpec(memory_space=pltpu.VMEM)
    results = pl.pallas_call(
        functools.partial(kernel_body, sizes),
        out_shape=[
            jax.ShapeDtypeStruct(field.shape, bf16),
            jax.ShapeDtypeStruct((tiles, C, CZ), f32),
            jax.ShapeDtypeStruct((8, HID), f32),
            jax.ShapeDtypeStruct((C, HID), f32),
        ],
        in_specs=[vmem] * 9,
        out_specs=[vmem] * 4,
        scratch_shapes=[
            pltpu.VMEM((CX + 2, CY + 2, C, CZ), bf16),
            pltpu.VMEM((CX + 2, CY + 2, C, CZ), bf16),
            pltpu.VMEM((CX + 2, CY + 2, 3 * C, CZ), bf16),
            pltpu.VMEM((CX + 2, CY + 2, 3 * C, CZ), bf16),
            pltpu.VMEM((2, C, CZ), bf16),
            pltpu.VMEM((2, 2, C, CZ), bf16),
            pltpu.VMEM((C, tiles * CZ), bf16),
            pltpu.VMEM((C, tiles * CZ), bf16),
            pltpu.VMEM((tiles, C, CZ), f32),
            pltpu.VMEM((CX, CY, C, CZ), f32),
            pltpu.VMEM((CY, C, CZ), f32),
            pltpu.VMEM((rows, CZ), bf16),
            pltpu.VMEM((nz - 1, rows // nz, CZ), bf16),
            pltpu.VMEM((rows // nz, CZ), bf16),
            pltpu.VMEM((nx * ny, rows // nz // ny, CZ), bf16),
            pltpu.VMEM((rows, CZ), bf16),
            dma((2, 8)), dma((2, 8)), dma((2, 2)), dma((2, 2)),
            dma((nz - 1,)), dma((nz - 1,)), dma((nx * ny - 1,)), dma((nx * ny - 1,)),
            dma((ny * nz - 1,)), dma((ny * nz - 1,)),
        ],
        compiler_params=pltpu.CompilerParams(
            collective_id=0, has_side_effects=True, vmem_limit_bytes=32 * 1024 * 1024
        ),
    )(
        field,
        cotangent,
        cosmology[None],
        lift_weight,
        lift_bias[None],
        style_weight.T,
        style_bias[None],
        jnp.transpose(kernel, (2, 3, 4, 0, 1)).reshape(taps, C, C),
        offset[None],
    )
    grad, grad_kernel, grad_offset, grad_lift, grad_liftbias, grad_style_t, grad_stylebias = (
        pl.pallas_call(
            hand_out,
            out_shape=[
                jax.ShapeDtypeStruct(field.shape, bf16),
                jax.ShapeDtypeStruct((taps, C, C), f32),
                jax.ShapeDtypeStruct((1, C), f32),
                jax.ShapeDtypeStruct(lift_weight.shape, f32),
                jax.ShapeDtypeStruct((1, HID), f32),
                jax.ShapeDtypeStruct((C, HID), f32),
                jax.ShapeDtypeStruct((1, C), f32),
            ],
            in_specs=[vmem] * 4,
            out_specs=[vmem] * 7,
            compiler_params=pltpu.CompilerParams(vmem_limit_bytes=8 * 1024 * 1024),
        )(*results)
    )
    return (
        grad,
        jnp.transpose(grad_kernel.reshape(kernel.shape[2:] + (C, C)), (3, 4, 0, 1, 2)),
        grad_offset[0],
        grad_lift,
        grad_liftbias[0],
        grad_style_t.T,
        grad_stylebias[0],
    )


def solution(mesh):
    sizes = (mesh.shape["gx"], mesh.shape["gy"], mesh.shape["gz"])
    placed = P(None, "gx", "gy", "gz")
    return jax.shard_map(
        functools.partial(body, sizes),
        mesh=mesh,
        in_specs=(placed, placed, P(), P(), P(), P(), P(), P(), P()),
        out_specs=(placed, P(), P(), P(), P(), P(), P()),
        check_vma=False,
    )
```

```python
import functools

import jax
import jax.numpy as jnp
from jax import lax
from jax.experimental import pallas as pl
from jax.experimental.pallas import tpu as pltpu
from jax.sharding import PartitionSpec as P

demod_eps = 1e-06
clip_eps = 1e-06
MESH = pl.DeviceIdType.MESH
SIDES = tuple((dx, dy) for dx in (-1, 0, 1) for dy in (-1, 0, 1) if (dx, dy) != (0, 0))


def silu_slope(values):
    logistic = 1.0 / (1.0 + jnp.exp(-values))
    return logistic * (1.0 + values * (1.0 - logistic))


def kernel_body(
    sizes,
    field_hbm, cotangent_hbm, cosmology_hbm, lift_weight_hbm, lift_bias_hbm, style_hbm,
    style_bias_hbm, kernel_hbm, offset_hbm,
    grad, grad_packed, grad_rows, grad_style_t,
    field, cotangent, cosmology, lift_weight, lift_bias, style_t, style_bias, kernel, offset,
    fetch_sem, field_ext, up_ext, field_taps, up_taps, edge_out, edge_in, w_fwd, w_bwd, packed, cot, turned_back,
    share, from_z, part_z, from_xy, total,
    xy_send, xy_recv, z_send, z_recv, rz_send, rz_recv, rxy_send, rxy_recv, g_send, g_recv,
):
    nx, ny, nz = sizes
    C, CX, CY, CZ = field.shape
    EY = CY + 2
    taps = kernel.shape[0]
    per = CZ // C
    tiles = (taps + per) // per
    fetches = [
        pltpu.make_async_copy(source, held, fetch_sem.at[k])
        for k, (source, held) in enumerate(
            zip(
                (field_hbm, kernel_hbm, cosmology_hbm, lift_weight_hbm, lift_bias_hbm, style_hbm,
                 style_bias_hbm, offset_hbm, cotangent_hbm),
                (field, kernel, cosmology, lift_weight, lift_bias, style_t, style_bias, offset,
                 cotangent),
            )
        )
    ]
    for fetch in fetches:
        fetch.start()
    me_x, me_y, me_z = (lax.axis_index("gx"), lax.axis_index("gy"), lax.axis_index("gz"))

    def at(dx=0, dy=0, dz=0):
        return (
            lax.rem(me_x + (dx + nx), nx) if dx else me_x,
            lax.rem(me_y + (dy + ny), ny) if dy else me_y,
            lax.rem(me_z + (dz + nz), nz) if dz else me_z,
        )

    plane_xy = [(dx, dy) for dx in range(nx) for dy in range(ny) if (dx, dy) != (0, 0)]
    plane_yz = [(dy, dz) for dy in range(ny) for dz in range(nz) if (dy, dz) != (0, 0)]
    edge_dx = (0, 1) if nx == 2 else (-1, 0, 1)
    corners = [(dx, dy, dz) for dz in (1, -1) for dx in edge_dx for dy in (-1, 0, 1)]
    steps = {}
    for dx, dy, dz in (
        [(dx, dy, 0) for dx, dy in SIDES + tuple(plane_xy)]
        + [(0, dy, dz) for dy, dz in plane_yz]
        + corners
    ):
        steps[(dx % nx, dy % ny, dz % nz)] = True
    partners = [at(*step) for step in steps]
    barrier = pltpu.get_barrier_semaphore()
    for partner in partners:
        pl.semaphore_signal(barrier, inc=1, device_id=partner, device_id_type=MESH)

    def remote(src, dst, send, recv, device):
        return pltpu.make_async_remote_copy(
            src_ref=src, dst_ref=dst, send_sem=send, recv_sem=recv, device_id=device,
            device_id_type=MESH,
        )

    def span(step, count, first):
        if step == 0:
            return pl.ds(first, count), pl.ds(1, count)
        if step > 0:
            return pl.ds(first + count - 1, 1), pl.ds(0, 1)
        return pl.ds(first, 1), pl.ds(count + 1, 1)

    def side_copies(which, source, first, ext):
        copies = []
        for at_side, (dx, dy) in enumerate(SIDES):
            sx, tx = span(dx, CX, first)
            sy, ty = span(dy, CY, first)
            copies.append(
                remote(source.at[sx, sy], ext.at[tx, ty], xy_send.at[which, at_side],
                       xy_recv.at[which, at_side], at(dx, dy))
            )
        return copies

    lanes = lax.broadcasted_iota(jnp.int32, (C, CZ), 1)
    group = lax.div(lanes, 2)

    def edge_copies(which):
        return [
            remote(edge_out.at[which],
                   edge_in.at[which, 0 if dz > 0 else 1, 1 - dx, 1 - dy],
                   z_send.at[which, k], z_recv.at[which, k], at(dx, dy, dz))
            for k, (dx, dy, dz) in enumerate(corners)
        ]

    def pack_edges(which, ext):
        edges = jnp.zeros((C, CZ), jnp.float32)
        for x in range(CX):
            for y in range(CY):
                row = x * CY + y
                rolled = pltpu.roll(ext[x + 1, y + 1].astype(jnp.float32), 1 + 2 * row, 1)
                edges = jnp.where(group == row, rolled, edges)
        edge_out[which] = edges.astype(jnp.bfloat16)

    def build_taps(which, ext, out):
        def plane(p, carry):
            first, final = p == 0, p == CX + 1
            place_x = jnp.where(first, 0, jnp.where(final, 0 if nx == 2 else 2, 1))
            x = jnp.where(first, CX - 1, jnp.where(final, 0, p - 1))
            tiles_at = {}
            for y in range(EY):
                place_y, line = (0, CY - 1) if y == 0 else (2, 0) if y == EY - 1 else (1, y - 1)
                if place_y not in tiles_at:
                    tiles_at[place_y] = [
                        edge_in[which, side, place_x, place_y].astype(jnp.float32)
                        for side in (0, 1)
                    ]
                before, after = tiles_at[place_y]
                row = x * CY + line
                mid = ext[p, y]
                wide = mid.astype(jnp.float32)
                low = jnp.where(lanes == 0, pltpu.roll(before, lax.rem(CZ - 2 * row, CZ), 1),
                                pltpu.roll(wide, 1, 1))
                high = jnp.where(lanes == CZ - 1, pltpu.roll(after, CZ - 2 - 2 * row, 1),
                                 pltpu.roll(wide, CZ - 1, 1))
                out[p, y, 0:C] = low.astype(jnp.bfloat16)
                out[p, y, C : 2 * C] = mid
                out[p, y, 2 * C : 3 * C] = high.astype(jnp.bfloat16)
            return carry

        lax.fori_loop(0, CX + 2, plane, 0)

    def columns(source, p, y):
        return jnp.concatenate(
            [source[p, pl.ds(y + k, 3)].reshape(9 * C, CZ) for k in range(2)], axis=1
        )

    def convolve(weights, source, y):
        results = [None] * CX
        for p in range(CX + 2):
            product = jnp.dot(weights[...], columns(source, p, y),
                              preferred_element_type=jnp.float32)
            for a in range(3):
                if 0 <= p - a < CX:
                    term = product[a * C : (a + 1) * C]
                    results[p - a] = term if results[p - a] is None else results[p - a] + term
        return results

    fetches[0].wait()
    for x in range(CX):
        turned_x = jnp.swapaxes(field[:, x].astype(jnp.float32), 0, 1)
        field_ext[x + 1, 1 : CY + 1] = turned_x.astype(jnp.bfloat16)
    pack_edges(0, field_ext)
    pl.semaphore_wait(barrier, len(partners))
    field_sides = side_copies(0, field_ext, 1, field_ext) + edge_copies(0)
    for copy in field_sides:
        copy.start()
    for fetch in fetches[1:]:
        fetch.wait()

    eye = lax.broadcasted_iota(jnp.int32, (C, C), 0) == lax.broadcasted_iota(jnp.int32, (C, C), 1)

    def to_row(column):
        return jnp.sum(jnp.where(eye, column, 0.0), axis=0, keepdims=True)

    def to_column(row):
        return jnp.sum(jnp.where(eye, row, 0.0), axis=1, keepdims=True)

    lifted = lift_bias[...]
    for k in range(lift_weight.shape[0]):
        lifted = lifted + cosmology[0:1, k : k + 1] * lift_weight[k : k + 1, :]
    hidden = lifted / (1.0 + jnp.exp(-lifted))
    styles_column = (
        jnp.sum(style_t[...] * hidden, axis=1, keepdims=True) + to_column(style_bias[...]) + 1.0
    )
    styles = to_row(styles_column)
    styles_wide = jnp.concatenate([styles] * per, axis=1)
    squares = jnp.zeros((C, CZ), jnp.float32)
    for j in range(tiles):
        members = [
            kernel[per * j + k] if per * j + k < taps else jnp.zeros((C, C), jnp.float32)
            for k in range(per)
        ]
        tile = jnp.concatenate(members, axis=1)
        packed[j] = tile
        modded = tile * styles_wide
        squares = squares + modded * modded
    inv_norm = lax.rsqrt(jnp.sum(squares, axis=1, keepdims=True) + demod_eps)
    turned = []
    for j in range(tiles):
        flat = (packed[j] * styles_wide * inv_norm).T
        turned += [flat[k * C : (k + 1) * C] for k in range(per)]
    turned = turned[:taps][::-1]
    for a in range(3):
        taken = range(9 * a, 9 * a + 9)
        w_fwd[a * C : (a + 1) * C, :] = jnp.concatenate(
            [kernel[t] * styles * inv_norm for t in taken], axis=1
        ).astype(jnp.bfloat16)
        w_bwd[a * C : (a + 1) * C, :] = jnp.concatenate(
            [turned[t] for t in taken], axis=1
        ).astype(jnp.bfloat16)
    offset_column = to_column(offset[...])
    for x in range(CX):
        cot[x] = jnp.swapaxes(cotangent[:, x].astype(jnp.float32), 0, 1)

    for copy in field_sides:
        copy.wait()
    build_taps(0, field_ext, field_taps)

    depth = taps * C

    def forward(at_pair, carry):
        y = 2 * at_pair
        for x, sums in enumerate(convolve(w_fwd, field_taps, y)):
            above = jnp.concatenate([cot[x, y], cot[x, y + 1]], axis=1)
            upstream = (above * silu_slope(sums + offset_column)).astype(jnp.bfloat16)
            up_ext[x + 1, y + 1] = upstream[:, :CZ]
            up_ext[x + 1, y + 2] = upstream[:, CZ:]
        return carry

    lax.fori_loop(0, CY // 2, forward, 0)
    pack_edges(1, up_ext)
    up_sides = side_copies(1, up_ext, 1, up_ext) + edge_copies(1)
    for copy in up_sides:
        copy.start()

    def weigh(at_pair, carry):
        y = 2 * at_pair
        sums, offsets = list(carry[:3]), carry[3]
        ups = []
        for x in range(CX):
            upstream = jnp.concatenate([up_ext[x + 1, y + 1], up_ext[x + 1, y + 2]], axis=1)
            wide = upstream.astype(jnp.float32)
            offsets = offsets + wide[:, :CZ] + wide[:, CZ:]
            ups.append(upstream)
        for p in range(CX + 2):
            taken = [a for a in range(3) if 0 <= p - a < CX]
            product = lax.dot_general(
                jnp.concatenate([ups[p - a] for a in taken], axis=0),
                columns(field_taps, p, y), (((1,), (1,)), ((), ())),
                preferred_element_type=jnp.float32,
            )
            for k, a in enumerate(taken):
                sums[a] = sums[a] + product[k * C : (k + 1) * C]
        return (*sums, offsets)

    *sums, offsets = lax.fori_loop(
        0, CY // 2, weigh,
        (jnp.zeros((C, 9 * C), jnp.float32),) * 3 + (jnp.zeros((C, CZ), jnp.float32),),
    )
    sums = jnp.concatenate(sums, axis=1)
    offset_sum = jnp.sum(offsets, axis=1, keepdims=True)
    for j in range(share.shape[0] // C):
        if (j + 1) * CZ <= depth:
            tile = sums[:, j * CZ : (j + 1) * CZ]
        elif j < tiles:
            used = depth - j * CZ
            tile = jnp.concatenate(
                [sums[:, j * CZ : depth], jnp.broadcast_to(offset_sum, (C, CZ - used))], axis=1
            )
        else:
            tile = jnp.zeros((C, CZ), jnp.float32)
        share[j * C : (j + 1) * C] = tile.astype(jnp.bfloat16)

    rows_z = share.shape[0] // nz
    rows_y = rows_z // ny

    def rows_at(base, count):
        return pl.ds(pl.multiple_of(base, 16), count)

    reduce_z = []
    for k in range(1, nz):
        there = at(dz=k)
        reduce_z.append(remote(share.at[rows_at(there[2] * rows_z, rows_z)], from_z.at[k - 1],
                               rz_send.at[k - 1], rz_recv.at[k - 1], there))
    for copy in reduce_z:
        copy.start()

    for copy in reduce_z:
        copy.wait()
    mine = share[rows_at(me_z * rows_z, rows_z), :].astype(jnp.float32)
    for k in range(1, nz):
        mine = mine + from_z[k - 1].astype(jnp.float32)
    part_z[...] = mine.astype(jnp.bfloat16)
    my_slot = me_x * ny + me_y
    reduce_xy = []
    for k, (dx, dy) in enumerate(plane_xy):
        there = at(dx, dy)
        reduce_xy.append(remote(part_z.at[rows_at(there[1] * rows_y, rows_y)], from_xy.at[my_slot],
                                rxy_send.at[k], rxy_recv.at[k], there))
    for copy in reduce_xy:
        copy.start()
    from_xy[my_slot] = part_z[rows_at(me_y * rows_y, rows_y), :]

    for copy in up_sides:
        copy.wait()
    build_taps(1, up_ext, up_taps)

    def backward(at_pair, carry):
        y = 2 * at_pair
        for x, result in enumerate(convolve(w_bwd, up_taps, y)):
            turned_back[x, y] = result[:, :CZ]
            turned_back[x, y + 1] = result[:, CZ:]
        return carry

    middle = CY // 4
    lax.fori_loop(0, middle, backward, 0)

    for copy in reduce_xy:
        copy.wait()
    mine = from_xy[0].astype(jnp.float32)
    for k in range(1, nx * ny):
        mine = mine + from_xy[k].astype(jnp.float32)
    own = rows_at(me_z * rows_z + me_y * rows_y, rows_y)
    total[own, :] = mine.astype(jnp.bfloat16)
    gather = [
        remote(total.at[own], total.at[own], g_send.at[k], g_recv.at[k], at(0, dy, dz))
        for k, (dy, dz) in enumerate(plane_yz)
    ]
    for copy in gather:
        copy.start()
    lax.fori_loop(middle, CY // 2, backward, 0)
    for x in range(CX):
        grad[:, x] = jnp.swapaxes(turned_back[x], 0, 1).astype(jnp.bfloat16)
    for copy in gather:
        copy.wait()

    last = taps - per * (tiles - 1)
    projected = jnp.zeros((C, CZ), jnp.float32)
    sum_tiles, modded_tiles = [], []
    for j in range(tiles):
        tile = total[j * C : (j + 1) * C, :].astype(jnp.float32)
        if j == tiles - 1:
            offset_row = to_row(tile[:, last * C : last * C + 1])
            tile = jnp.where(lanes < last * C, tile, 0.0)
        modded = packed[j] * styles_wide
        projected = projected + tile * modded
        sum_tiles.append(tile)
        modded_tiles.append(modded)
    projected = jnp.sum(projected, axis=1, keepdims=True)
    scale = inv_norm * inv_norm * projected
    raws = []
    square = jnp.zeros((C, CZ), jnp.float32)
    along = jnp.zeros((C, CZ), jnp.float32)
    for j in range(tiles):
        mod_grad = inv_norm * (sum_tiles[j] - modded_tiles[j] * scale)
        raw = mod_grad * styles_wide
        along = along + mod_grad * packed[j]
        square = square + raw * raw
        raws.append(raw)
    along = jnp.sum(along, axis=0, keepdims=True)
    styles_grad = along[:, 0:C]
    for k in range(1, per):
        styles_grad = styles_grad + along[:, k * C : (k + 1) * C]
    styles_grad_column = to_column(styles_grad)
    hidden_grad = jnp.sum(style_t[...] * styles_grad_column, axis=0, keepdims=True)
    lifted_grad = hidden_grad * silu_slope(lifted)
    style_raw = styles_grad_column * hidden
    lift_raws = [
        cosmology[0:1, k : k + 1] * lifted_grad for k in range(lift_weight.shape[0])
    ]

    def sum_all(values):
        return jnp.sum(jnp.sum(values, axis=1, keepdims=True), axis=0, keepdims=True)

    square_sum = sum_all(square)
    for member in [offset_row, lifted_grad, style_raw, styles_grad] + lift_raws:
        square_sum = square_sum + sum_all(member * member)
    entries = taps * C * C + 2 * C + (1 + lift_weight.shape[0] + C) * lifted.shape[1]
    factor = jnp.minimum(1.0, lax.rsqrt(square_sum / entries + clip_eps))
    for j in range(tiles):
        grad_packed[j] = raws[j] * factor
    grad_style_t[...] = style_raw * factor
    wide = lifted.shape[1]
    small = jnp.concatenate([offset_row, styles_grad], axis=1)
    grad_rows[0:1, 0 : 2 * C] = small * factor
    grad_rows[1:2, :] = lifted_grad * factor
    for k in range(lift_weight.shape[0]):
        grad_rows[k + 2 : k + 3, :] = lift_raws[k] * factor


def hand_out(
    grad_in, grad_packed, grad_rows, grad_style_in,
    grad, grad_kernel, grad_offset, grad_lift, grad_liftbias, grad_style_t, grad_stylebias,
):
    C = grad_packed.shape[1]
    per = grad_packed.shape[2] // C
    grad[...] = grad_in[...]
    for t in range(grad_kernel.shape[0]):
        k = t % per
        grad_kernel[t] = grad_packed[t // per][:, k * C : (k + 1) * C]
    grad_offset[...] = grad_rows[0:1, 0:C]
    grad_stylebias[...] = grad_rows[0:1, C : 2 * C]
    grad_liftbias[...] = grad_rows[1:2, :]
    grad_lift[...] = grad_rows[2 : 2 + grad_lift.shape[0], :]
    grad_style_t[...] = grad_style_in[...]


def body(
    sizes, field, cotangent, cosmology, lift_weight, lift_bias, style_weight, style_bias, kernel,
    offset,
):
    nx, ny, nz = sizes
    C, CX, CY, CZ = field.shape
    HID = lift_bias.shape[0]
    taps = kernel.shape[2] * kernel.shape[3] * kernel.shape[4]
    per = CZ // C
    tiles = (taps + per) // per
    unit = nz * ny * 16
    rows = -(-tiles * C // unit) * unit
    f32, bf16 = jnp.float32, jnp.bfloat16
    dma = pltpu.SemaphoreType.DMA
    vmem = pl.BlockSpec(memory_space=pltpu.VMEM)
    results = pl.pallas_call(
        functools.partial(kernel_body, sizes),
        out_shape=[
            jax.ShapeDtypeStruct(field.shape, bf16),
            jax.ShapeDtypeStruct((tiles, C, CZ), f32),
            jax.ShapeDtypeStruct((8, HID), f32),
            jax.ShapeDtypeStruct((C, HID), f32),
        ],
        in_specs=[pl.BlockSpec(memory_space=pltpu.HBM)] * 9,
        out_specs=[vmem] * 4,
        scratch_shapes=[
            pltpu.VMEM(field.shape, bf16),
            pltpu.VMEM(field.shape, bf16),
            pltpu.VMEM((1, cosmology.shape[0]), f32),
            pltpu.VMEM(lift_weight.shape, f32),
            pltpu.VMEM((1, HID), f32),
            pltpu.VMEM((C, HID), f32),
            pltpu.VMEM((1, C), f32),
            pltpu.VMEM((taps, C, C), f32),
            pltpu.VMEM((1, C), f32),
            dma((9,)),
            pltpu.VMEM((CX + 2, CY + 2, C, CZ), bf16),
            pltpu.VMEM((CX + 2, CY + 2, C, CZ), bf16),
            pltpu.VMEM((CX + 2, CY + 2, 3 * C, CZ), bf16),
            pltpu.VMEM((CX + 2, CY + 2, 3 * C, CZ), bf16),
            pltpu.VMEM((2, C, CZ), bf16),
            pltpu.VMEM((2, 2, 3, 3, C, CZ), bf16),
            pltpu.VMEM((3 * C, 9 * C), bf16),
            pltpu.VMEM((3 * C, 9 * C), bf16),
            pltpu.VMEM((tiles, C, CZ), f32),
            pltpu.VMEM((CX, CY, C, CZ), f32),
            pltpu.VMEM((CX, CY, C, CZ), f32),
            pltpu.VMEM((rows, CZ), bf16),
            pltpu.VMEM((nz - 1, rows // nz, CZ), bf16),
            pltpu.VMEM((rows // nz, CZ), bf16),
            pltpu.VMEM((nx * ny, rows // nz // ny, CZ), bf16),
            pltpu.VMEM((rows, CZ), bf16),
            dma((2, 8)), dma((2, 8)), dma((2, 18)), dma((2, 18)),
            dma((nz - 1,)), dma((nz - 1,)), dma((nx * ny - 1,)), dma((nx * ny - 1,)),
            dma((ny * nz - 1,)), dma((ny * nz - 1,)),
        ],
        compiler_params=pltpu.CompilerParams(
            collective_id=0, has_side_effects=True, vmem_limit_bytes=60 * 1024 * 1024
        ),
    )(
        field,
        cotangent,
        cosmology[None],
        lift_weight,
        lift_bias[None],
        style_weight.T,
        style_bias[None],
        jnp.transpose(kernel, (2, 3, 4, 0, 1)).reshape(taps, C, C),
        offset[None],
    )
    grad, grad_kernel, grad_offset, grad_lift, grad_liftbias, grad_style_t, grad_stylebias = (
        pl.pallas_call(
            hand_out,
            out_shape=[
                jax.ShapeDtypeStruct(field.shape, bf16),
                jax.ShapeDtypeStruct((taps, C, C), f32),
                jax.ShapeDtypeStruct((1, C), f32),
                jax.ShapeDtypeStruct(lift_weight.shape, f32),
                jax.ShapeDtypeStruct((1, HID), f32),
                jax.ShapeDtypeStruct((C, HID), f32),
                jax.ShapeDtypeStruct((1, C), f32),
            ],
            in_specs=[vmem] * 4,
            out_specs=[vmem] * 7,
            compiler_params=pltpu.CompilerParams(vmem_limit_bytes=60 * 1024 * 1024),
        )(*results)
    )
    return (
        grad,
        jnp.transpose(grad_kernel.reshape(kernel.shape[2:] + (C, C)), (3, 4, 0, 1, 2)),
        grad_offset[0],
        grad_lift,
        grad_liftbias[0],
        grad_style_t.T,
        grad_stylebias[0],
    )


def solution(mesh):
    sizes = (mesh.shape["gx"], mesh.shape["gy"], mesh.shape["gz"])
    placed = P(None, "gx", "gy", "gz")
    return jax.shard_map(
        functools.partial(body, sizes),
        mesh=mesh,
        in_specs=(placed, placed, P(), P(), P(), P(), P(), P(), P()),
        out_specs=(placed, P(), P(), P(), P(), P(), P()),
        check_vma=False,
    )
```

```python
import functools

import jax
import jax.numpy as jnp
from jax import lax
from jax.experimental import pallas as pl
from jax.experimental.pallas import tpu as pltpu
from jax.sharding import PartitionSpec as P

demod_eps = 1e-06
clip_eps = 1e-06
MESH = pl.DeviceIdType.MESH
SIDES = tuple((dx, dy) for dx in (-1, 0, 1) for dy in (-1, 0, 1) if (dx, dy) != (0, 0))


def silu_slope(values):
    logistic = 1.0 / (1.0 + jnp.exp(-values))
    return logistic * (1.0 + values * (1.0 - logistic))


def kernel_body(
    sizes,
    field_hbm, cotangent_hbm, cosmology_hbm, lift_weight_hbm, lift_bias_hbm, style_hbm,
    style_bias_hbm, kernel_hbm, offset_hbm,
    grad, grad_packed, grad_rows, grad_style_t,
    field, cotangent, cosmology, lift_weight, lift_bias, style_t, style_bias, kernel, offset,
    fetch_sem, field_ext, up_ext, field_taps, up_taps, edge_out, edge_in, w_fwd, w_bwd, packed, cot, turned_back, held,
    share, from_z, part_z, from_xy, total,
    xy_send, xy_recv, z_send, z_recv, rz_send, rz_recv, rxy_send, rxy_recv, g_send, g_recv,
):
    nx, ny, nz = sizes
    C, CX, CY, CZ = field.shape
    EY = CY + 2
    taps = kernel.shape[0]
    per = CZ // C
    tiles = (taps + per) // per
    fetches = [
        pltpu.make_async_copy(source, there, fetch_sem.at[k])
        for k, (source, there) in enumerate(
            zip(
                (field_hbm, kernel_hbm, cosmology_hbm, lift_weight_hbm, lift_bias_hbm, style_hbm,
                 style_bias_hbm, offset_hbm, cotangent_hbm),
                (field, kernel, cosmology, lift_weight, lift_bias, style_t, style_bias, offset,
                 cotangent),
            )
        )
    ]
    for fetch in fetches:
        fetch.start()
    me_x, me_y, me_z = (lax.axis_index("gx"), lax.axis_index("gy"), lax.axis_index("gz"))

    def at(dx=0, dy=0, dz=0):
        return (
            lax.rem(me_x + (dx + nx), nx) if dx else me_x,
            lax.rem(me_y + (dy + ny), ny) if dy else me_y,
            lax.rem(me_z + (dz + nz), nz) if dz else me_z,
        )

    plane_xy = [(dx, dy) for dx in range(nx) for dy in range(ny) if (dx, dy) != (0, 0)]
    plane_yz = [(dy, dz) for dy in range(ny) for dz in range(nz) if (dy, dz) != (0, 0)]
    edge_dx = (0, 1) if nx == 2 else (-1, 0, 1)
    corners = [(dx, dy, dz) for dz in (1, -1) for dx in edge_dx for dy in (-1, 0, 1)]
    steps = {}
    for dx, dy, dz in (
        [(dx, dy, 0) for dx, dy in SIDES + tuple(plane_xy)]
        + [(0, dy, dz) for dy, dz in plane_yz]
        + corners
    ):
        steps[(dx % nx, dy % ny, dz % nz)] = True
    partners = [at(*step) for step in steps]
    barrier = pltpu.get_barrier_semaphore()
    for partner in partners:
        pl.semaphore_signal(barrier, inc=1, device_id=partner, device_id_type=MESH)

    def remote(src, dst, send, recv, device):
        return pltpu.make_async_remote_copy(
            src_ref=src, dst_ref=dst, send_sem=send, recv_sem=recv, device_id=device,
            device_id_type=MESH,
        )

    def span(step, count, first):
        if step == 0:
            return pl.ds(first, count), pl.ds(1, count)
        if step > 0:
            return pl.ds(first + count - 1, 1), pl.ds(0, 1)
        return pl.ds(first, 1), pl.ds(count + 1, 1)

    def side_copies(which, ext, near):
        copies = []
        for at_side, (dx, dy) in enumerate(SIDES):
            if (dx == 0) == near:
                sx, tx = span(dx, CX, 1)
                sy, ty = span(dy, CY, 1)
                copies.append(
                    remote(ext.at[sx, sy], ext.at[tx, ty], xy_send.at[which, at_side],
                           xy_recv.at[which, at_side], at(dx, dy))
                )
        return copies

    lanes = lax.broadcasted_iota(jnp.int32, (C, CZ), 1)
    group = lax.div(lanes, 2)

    def edge_copies(which, near):
        return [
            remote(edge_out.at[which],
                   edge_in.at[which, 0 if dz > 0 else 1, 1 - dx, 1 - dy],
                   z_send.at[which, k], z_recv.at[which, k], at(dx, dy, dz))
            for k, (dx, dy, dz) in enumerate(corners)
            if (dx == 0) == near
        ]

    def exchange(which, ext):
        near = side_copies(which, ext, True) + edge_copies(which, True)
        far = side_copies(which, ext, False) + edge_copies(which, False)
        for copy in near + far:
            copy.start()
        return near, far

    def pack_edges(which, ext):
        edges = jnp.zeros((C, CZ), jnp.float32)
        for x in range(CX):
            for y in range(CY):
                row = x * CY + y
                rolled = pltpu.roll(ext[x + 1, y + 1].astype(jnp.float32), 1 + 2 * row, 1)
                edges = jnp.where(group == row, rolled, edges)
        edge_out[which] = edges.astype(jnp.bfloat16)

    def build_taps(which, ext, out, p, place_x, x):
        tiles_at = {}
        for y in range(EY):
            place_y, line = (0, CY - 1) if y == 0 else (2, 0) if y == EY - 1 else (1, y - 1)
            if place_y not in tiles_at:
                tiles_at[place_y] = [
                    edge_in[which, side, place_x, place_y].astype(jnp.float32)
                    for side in (0, 1)
                ]
            before, after = tiles_at[place_y]
            row = x * CY + line
            mid = ext[p, y]
            wide = mid.astype(jnp.float32)
            low = jnp.where(lanes == 0, pltpu.roll(before, lax.rem(CZ - 2 * row, CZ), 1),
                            pltpu.roll(wide, 1, 1))
            high = jnp.where(lanes == CZ - 1, pltpu.roll(after, CZ - 2 - 2 * row, 1),
                             pltpu.roll(wide, CZ - 1, 1))
            out[p, y, 0:C] = low.astype(jnp.bfloat16)
            out[p, y, C : 2 * C] = mid
            out[p, y, 2 * C : 3 * C] = high.astype(jnp.bfloat16)

    def build_near(which, ext, out):
        def plane(x, carry):
            build_taps(which, ext, out, x + 1, 1, x)
            return carry

        lax.fori_loop(0, CX, plane, 0)

    def build_far(which, ext, out):
        build_taps(which, ext, out, 0, 0, CX - 1)
        build_taps(which, ext, out, CX + 1, 0 if nx == 2 else 2, 0)

    def columns(source, p, y):
        return jnp.concatenate(
            [source[p, pl.ds(y + k, 3)].reshape(9 * C, CZ) for k in range(2)], axis=1
        )

    near_planes, far_planes = range(1, CX + 1), (0, CX + 1)

    def convolve(weights, source, y, planes, results):
        for p in planes:
            taken = [a for a in range(3) if 0 <= p - a < CX]
            product = jnp.dot(weights[taken[0] * C : (taken[-1] + 1) * C, :],
                              columns(source, p, y), preferred_element_type=jnp.float32)
            for k, a in enumerate(taken):
                term = product[k * C : (k + 1) * C]
                results[p - a] = term if results[p - a] is None else results[p - a] + term
        return results

    fetches[0].wait()
    for x in range(CX):
        turned_x = jnp.swapaxes(field[:, x].astype(jnp.float32), 0, 1)
        field_ext[x + 1, 1 : CY + 1] = turned_x.astype(jnp.bfloat16)
    pack_edges(0, field_ext)
    pl.semaphore_wait(barrier, len(partners))
    field_near, field_far = exchange(0, field_ext)
    for fetch in fetches[1:]:
        fetch.wait()

    eye = lax.broadcasted_iota(jnp.int32, (C, C), 0) == lax.broadcasted_iota(jnp.int32, (C, C), 1)

    def to_row(column):
        return jnp.sum(jnp.where(eye, column, 0.0), axis=0, keepdims=True)

    def to_column(row):
        return jnp.sum(jnp.where(eye, row, 0.0), axis=1, keepdims=True)

    lifted = lift_bias[...]
    for k in range(lift_weight.shape[0]):
        lifted = lifted + cosmology[0:1, k : k + 1] * lift_weight[k : k + 1, :]
    hidden = lifted / (1.0 + jnp.exp(-lifted))
    styles_column = (
        jnp.sum(style_t[...] * hidden, axis=1, keepdims=True) + to_column(style_bias[...]) + 1.0
    )
    styles = to_row(styles_column)
    styles_wide = jnp.concatenate([styles] * per, axis=1)
    squares = jnp.zeros((C, CZ), jnp.float32)
    for j in range(tiles):
        members = [
            kernel[per * j + k] if per * j + k < taps else jnp.zeros((C, C), jnp.float32)
            for k in range(per)
        ]
        tile = jnp.concatenate(members, axis=1)
        packed[j] = tile
        modded = tile * styles_wide
        squares = squares + modded * modded
    inv_norm = lax.rsqrt(jnp.sum(squares, axis=1, keepdims=True) + demod_eps)
    turned = []
    for j in range(tiles):
        flat = (packed[j] * styles_wide * inv_norm).T
        turned += [flat[k * C : (k + 1) * C] for k in range(per)]
    turned = turned[:taps][::-1]
    for a in range(3):
        taken = range(9 * a, 9 * a + 9)
        w_fwd[a * C : (a + 1) * C, :] = jnp.concatenate(
            [kernel[t] * styles * inv_norm for t in taken], axis=1
        ).astype(jnp.bfloat16)
        w_bwd[a * C : (a + 1) * C, :] = jnp.concatenate(
            [turned[t] for t in taken], axis=1
        ).astype(jnp.bfloat16)
    offset_column = to_column(offset[...])
    for x in range(CX):
        cot[x] = jnp.swapaxes(cotangent[:, x].astype(jnp.float32), 0, 1)

    for copy in field_near:
        copy.wait()
    build_near(0, field_ext, field_taps)

    depth = taps * C

    edge_x = sorted({0, CX - 1})

    def finish(x, y, sums):
        above = jnp.concatenate([cot[x, y], cot[x, y + 1]], axis=1)
        upstream = (above * silu_slope(sums + offset_column)).astype(jnp.bfloat16)
        up_ext[x + 1, y + 1] = upstream[:, :CZ]
        up_ext[x + 1, y + 2] = upstream[:, CZ:]

    def forward_near(at_pair, carry):
        y = 2 * at_pair
        results = convolve(w_fwd, field_taps, y, near_planes, [None] * CX)
        for x, sums in enumerate(results):
            if x in edge_x:
                held[x, at_pair] = sums
            else:
                finish(x, y, sums)
        return carry

    def forward_far(at_pair, carry):
        y = 2 * at_pair
        results = [held[x, at_pair] if x in edge_x else None for x in range(CX)]
        results = convolve(w_fwd, field_taps, y, far_planes, results)
        for x in edge_x:
            finish(x, y, results[x])
        return carry

    lax.fori_loop(0, CY // 2, forward_near, 0)
    for copy in field_far:
        copy.wait()
    build_far(0, field_ext, field_taps)
    lax.fori_loop(0, CY // 2, forward_far, 0)
    pack_edges(1, up_ext)
    up_near, up_far = exchange(1, up_ext)

    def weigh(at_pair, carry):
        y = 2 * at_pair
        sums, offsets = list(carry[:3]), carry[3]
        ups = []
        for x in range(CX):
            upstream = jnp.concatenate([up_ext[x + 1, y + 1], up_ext[x + 1, y + 2]], axis=1)
            wide = upstream.astype(jnp.float32)
            offsets = offsets + wide[:, :CZ] + wide[:, CZ:]
            ups.append(upstream)
        for p in range(CX + 2):
            taken = [a for a in range(3) if 0 <= p - a < CX]
            product = lax.dot_general(
                jnp.concatenate([ups[p - a] for a in taken], axis=0),
                columns(field_taps, p, y), (((1,), (1,)), ((), ())),
                preferred_element_type=jnp.float32,
            )
            for k, a in enumerate(taken):
                sums[a] = sums[a] + product[k * C : (k + 1) * C]
        return (*sums, offsets)

    *sums, offsets = lax.fori_loop(
        0, CY // 2, weigh,
        (jnp.zeros((C, 9 * C), jnp.float32),) * 3 + (jnp.zeros((C, CZ), jnp.float32),),
    )
    sums = jnp.concatenate(sums, axis=1)
    offset_sum = jnp.sum(offsets, axis=1, keepdims=True)
    for j in range(share.shape[0] // C):
        if (j + 1) * CZ <= depth:
            tile = sums[:, j * CZ : (j + 1) * CZ]
        elif j < tiles:
            used = depth - j * CZ
            tile = jnp.concatenate(
                [sums[:, j * CZ : depth], jnp.broadcast_to(offset_sum, (C, CZ - used))], axis=1
            )
        else:
            tile = jnp.zeros((C, CZ), jnp.float32)
        share[j * C : (j + 1) * C] = tile.astype(jnp.bfloat16)

    rows_z = share.shape[0] // nz
    rows_y = rows_z // ny

    def rows_at(base, count):
        return pl.ds(pl.multiple_of(base, 16), count)

    reduce_z = []
    for k in range(1, nz):
        there = at(dz=k)
        reduce_z.append(remote(share.at[rows_at(there[2] * rows_z, rows_z)], from_z.at[k - 1],
                               rz_send.at[k - 1], rz_recv.at[k - 1], there))
    for copy in reduce_z:
        copy.start()

    for copy in up_near:
        copy.wait()
    build_near(1, up_ext, up_taps)

    for copy in reduce_z:
        copy.wait()
    mine = share[rows_at(me_z * rows_z, rows_z), :].astype(jnp.float32)
    for k in range(1, nz):
        mine = mine + from_z[k - 1].astype(jnp.float32)
    part_z[...] = mine.astype(jnp.bfloat16)
    my_slot = me_x * ny + me_y
    reduce_xy = []
    for k, (dx, dy) in enumerate(plane_xy):
        there = at(dx, dy)
        reduce_xy.append(remote(part_z.at[rows_at(there[1] * rows_y, rows_y)], from_xy.at[my_slot],
                                rxy_send.at[k], rxy_recv.at[k], there))
    for copy in reduce_xy:
        copy.start()
    from_xy[my_slot] = part_z[rows_at(me_y * rows_y, rows_y), :]

    def backward_near(at_pair, carry):
        y = 2 * at_pair
        for x, sums in enumerate(convolve(w_bwd, up_taps, y, near_planes, [None] * CX)):
            held[x, at_pair] = sums
        return carry

    def backward_far(at_pair, carry):
        y = 2 * at_pair
        results = [held[x, at_pair] for x in range(CX)]
        for x, sums in enumerate(convolve(w_bwd, up_taps, y, far_planes, results)):
            turned_back[x, y] = sums[:, :CZ]
            turned_back[x, y + 1] = sums[:, CZ:]
        return carry

    lax.fori_loop(0, CY // 2, backward_near, 0)

    for copy in reduce_xy:
        copy.wait()
    mine = from_xy[0].astype(jnp.float32)
    for k in range(1, nx * ny):
        mine = mine + from_xy[k].astype(jnp.float32)
    own = rows_at(me_z * rows_z + me_y * rows_y, rows_y)
    total[own, :] = mine.astype(jnp.bfloat16)
    gather = [
        remote(total.at[own], total.at[own], g_send.at[k], g_recv.at[k], at(0, dy, dz))
        for k, (dy, dz) in enumerate(plane_yz)
    ]
    for copy in gather:
        copy.start()
    for copy in up_far:
        copy.wait()
    build_far(1, up_ext, up_taps)
    lax.fori_loop(0, CY // 2, backward_far, 0)
    for x in range(CX):
        grad[:, x] = jnp.swapaxes(turned_back[x], 0, 1).astype(jnp.bfloat16)
    for copy in gather:
        copy.wait()

    last = taps - per * (tiles - 1)
    projected = jnp.zeros((C, CZ), jnp.float32)
    sum_tiles, modded_tiles = [], []
    for j in range(tiles):
        tile = total[j * C : (j + 1) * C, :].astype(jnp.float32)
        if j == tiles - 1:
            offset_row = to_row(tile[:, last * C : last * C + 1])
            tile = jnp.where(lanes < last * C, tile, 0.0)
        modded = packed[j] * styles_wide
        projected = projected + tile * modded
        sum_tiles.append(tile)
        modded_tiles.append(modded)
    projected = jnp.sum(projected, axis=1, keepdims=True)
    scale = inv_norm * inv_norm * projected
    raws = []
    square = jnp.zeros((C, CZ), jnp.float32)
    along = jnp.zeros((C, CZ), jnp.float32)
    for j in range(tiles):
        mod_grad = inv_norm * (sum_tiles[j] - modded_tiles[j] * scale)
        raw = mod_grad * styles_wide
        along = along + mod_grad * packed[j]
        square = square + raw * raw
        raws.append(raw)
    along = jnp.sum(along, axis=0, keepdims=True)
    styles_grad = along[:, 0:C]
    for k in range(1, per):
        styles_grad = styles_grad + along[:, k * C : (k + 1) * C]
    styles_grad_column = to_column(styles_grad)
    hidden_grad = jnp.sum(style_t[...] * styles_grad_column, axis=0, keepdims=True)
    lifted_grad = hidden_grad * silu_slope(lifted)
    style_raw = styles_grad_column * hidden
    lift_raws = [
        cosmology[0:1, k : k + 1] * lifted_grad for k in range(lift_weight.shape[0])
    ]

    def sum_all(values):
        return jnp.sum(jnp.sum(values, axis=1, keepdims=True), axis=0, keepdims=True)

    square_sum = sum_all(square)
    for member in [offset_row, lifted_grad, style_raw, styles_grad] + lift_raws:
        square_sum = square_sum + sum_all(member * member)
    entries = taps * C * C + 2 * C + (1 + lift_weight.shape[0] + C) * lifted.shape[1]
    factor = jnp.minimum(1.0, lax.rsqrt(square_sum / entries + clip_eps))
    for j in range(tiles):
        grad_packed[j] = raws[j] * factor
    grad_style_t[...] = style_raw * factor
    wide = lifted.shape[1]
    small = jnp.concatenate([offset_row, styles_grad], axis=1)
    grad_rows[0:1, 0 : 2 * C] = small * factor
    grad_rows[1:2, :] = lifted_grad * factor
    for k in range(lift_weight.shape[0]):
        grad_rows[k + 2 : k + 3, :] = lift_raws[k] * factor


def hand_out(
    grad_in, grad_packed, grad_rows, grad_style_in,
    grad, grad_kernel, grad_offset, grad_lift, grad_liftbias, grad_style_t, grad_stylebias,
):
    C = grad_packed.shape[1]
    per = grad_packed.shape[2] // C
    grad[...] = grad_in[...]
    for t in range(grad_kernel.shape[0]):
        k = t % per
        grad_kernel[t] = grad_packed[t // per][:, k * C : (k + 1) * C]
    grad_offset[...] = grad_rows[0:1, 0:C]
    grad_stylebias[...] = grad_rows[0:1, C : 2 * C]
    grad_liftbias[...] = grad_rows[1:2, :]
    grad_lift[...] = grad_rows[2 : 2 + grad_lift.shape[0], :]
    grad_style_t[...] = grad_style_in[...]


def body(
    sizes, field, cotangent, cosmology, lift_weight, lift_bias, style_weight, style_bias, kernel,
    offset,
):
    nx, ny, nz = sizes
    C, CX, CY, CZ = field.shape
    HID = lift_bias.shape[0]
    taps = kernel.shape[2] * kernel.shape[3] * kernel.shape[4]
    per = CZ // C
    tiles = (taps + per) // per
    unit = nz * ny * 16
    rows = -(-tiles * C // unit) * unit
    f32, bf16 = jnp.float32, jnp.bfloat16
    dma = pltpu.SemaphoreType.DMA
    vmem = pl.BlockSpec(memory_space=pltpu.VMEM)
    results = pl.pallas_call(
        functools.partial(kernel_body, sizes),
        out_shape=[
            jax.ShapeDtypeStruct(field.shape, bf16),
            jax.ShapeDtypeStruct((tiles, C, CZ), f32),
            jax.ShapeDtypeStruct((8, HID), f32),
            jax.ShapeDtypeStruct((C, HID), f32),
        ],
        in_specs=[pl.BlockSpec(memory_space=pltpu.HBM)] * 9,
        out_specs=[vmem] * 4,
        scratch_shapes=[
            pltpu.VMEM(field.shape, bf16),
            pltpu.VMEM(field.shape, bf16),
            pltpu.VMEM((1, cosmology.shape[0]), f32),
            pltpu.VMEM(lift_weight.shape, f32),
            pltpu.VMEM((1, HID), f32),
            pltpu.VMEM((C, HID), f32),
            pltpu.VMEM((1, C), f32),
            pltpu.VMEM((taps, C, C), f32),
            pltpu.VMEM((1, C), f32),
            dma((9,)),
            pltpu.VMEM((CX + 2, CY + 2, C, CZ), bf16),
            pltpu.VMEM((CX + 2, CY + 2, C, CZ), bf16),
            pltpu.VMEM((CX + 2, CY + 2, 3 * C, CZ), bf16),
            pltpu.VMEM((CX + 2, CY + 2, 3 * C, CZ), bf16),
            pltpu.VMEM((2, C, CZ), bf16),
            pltpu.VMEM((2, 2, 3, 3, C, CZ), bf16),
            pltpu.VMEM((3 * C, 9 * C), bf16),
            pltpu.VMEM((3 * C, 9 * C), bf16),
            pltpu.VMEM((tiles, C, CZ), f32),
            pltpu.VMEM((CX, CY, C, CZ), f32),
            pltpu.VMEM((CX, CY, C, CZ), f32),
            pltpu.VMEM((CX, CY // 2, C, 2 * CZ), f32),
            pltpu.VMEM((rows, CZ), bf16),
            pltpu.VMEM((nz - 1, rows // nz, CZ), bf16),
            pltpu.VMEM((rows // nz, CZ), bf16),
            pltpu.VMEM((nx * ny, rows // nz // ny, CZ), bf16),
            pltpu.VMEM((rows, CZ), bf16),
            dma((2, 8)), dma((2, 8)), dma((2, 18)), dma((2, 18)),
            dma((nz - 1,)), dma((nz - 1,)), dma((nx * ny - 1,)), dma((nx * ny - 1,)),
            dma((ny * nz - 1,)), dma((ny * nz - 1,)),
        ],
        compiler_params=pltpu.CompilerParams(
            collective_id=0, has_side_effects=True, vmem_limit_bytes=60 * 1024 * 1024
        ),
    )(
        field,
        cotangent,
        cosmology[None],
        lift_weight,
        lift_bias[None],
        style_weight.T,
        style_bias[None],
        jnp.transpose(kernel, (2, 3, 4, 0, 1)).reshape(taps, C, C),
        offset[None],
    )
    grad, grad_kernel, grad_offset, grad_lift, grad_liftbias, grad_style_t, grad_stylebias = (
        pl.pallas_call(
            hand_out,
            out_shape=[
                jax.ShapeDtypeStruct(field.shape, bf16),
                jax.ShapeDtypeStruct((taps, C, C), f32),
                jax.ShapeDtypeStruct((1, C), f32),
                jax.ShapeDtypeStruct(lift_weight.shape, f32),
                jax.ShapeDtypeStruct((1, HID), f32),
                jax.ShapeDtypeStruct((C, HID), f32),
                jax.ShapeDtypeStruct((1, C), f32),
            ],
            in_specs=[vmem] * 4,
            out_specs=[vmem] * 7,
            compiler_params=pltpu.CompilerParams(vmem_limit_bytes=60 * 1024 * 1024),
        )(*results)
    )
    return (
        grad,
        jnp.transpose(grad_kernel.reshape(kernel.shape[2:] + (C, C)), (3, 4, 0, 1, 2)),
        grad_offset[0],
        grad_lift,
        grad_liftbias[0],
        grad_style_t.T,
        grad_stylebias[0],
    )


def solution(mesh):
    sizes = (mesh.shape["gx"], mesh.shape["gy"], mesh.shape["gz"])
    placed = P(None, "gx", "gy", "gz")
    return jax.shard_map(
        functools.partial(body, sizes),
        mesh=mesh,
        in_specs=(placed, placed, P(), P(), P(), P(), P(), P(), P()),
        out_specs=(placed, P(), P(), P(), P(), P(), P()),
        check_vma=False,
    )
```

```python
import functools

import jax
import jax.numpy as jnp
from jax import lax
from jax.experimental import pallas as pl
from jax.experimental.pallas import tpu as pltpu
from jax.sharding import PartitionSpec as P

demod_eps = 1e-06
clip_eps = 1e-06
MESH = pl.DeviceIdType.MESH
SIDES = tuple((dx, dy) for dx in (-1, 0, 1) for dy in (-1, 0, 1) if (dx, dy) != (0, 0))


def silu_slope(values):
    logistic = 1.0 / (1.0 + jnp.exp(-values))
    return logistic * (1.0 + values * (1.0 - logistic))


def kernel_body(
    sizes,
    field_hbm, cotangent_hbm, cosmology_hbm, lift_weight_hbm, lift_bias_hbm, style_hbm,
    style_bias_hbm, kernel_hbm, offset_hbm,
    grad, grad_packed, grad_rows, grad_style_t,
    field, cotangent, cosmology, lift_weight, lift_bias, style_t, style_bias, kernel, offset,
    fetch_sem, field_ext, up_ext, field_taps, up_taps, edge_out, edge_in, w_fwd, w_bwd, packed, cot, turned_back, held,
    share, from_z, part_z, from_xy, total,
    xy_send, xy_recv, z_send, z_recv, rz_send, rz_recv, rxy_send, rxy_recv, g_send, g_recv,
):
    nx, ny, nz = sizes
    C, CX, CY, CZ = field.shape
    EY = CY + 2
    taps = kernel.shape[0]
    per = CZ // C
    tiles = (taps + per) // per
    fetches = [
        pltpu.make_async_copy(source, there, fetch_sem.at[k])
        for k, (source, there) in enumerate(
            zip(
                (field_hbm, kernel_hbm, cosmology_hbm, lift_weight_hbm, lift_bias_hbm, style_hbm,
                 style_bias_hbm, offset_hbm, cotangent_hbm),
                (field, kernel, cosmology, lift_weight, lift_bias, style_t, style_bias, offset,
                 cotangent),
            )
        )
    ]
    fetches[0].start()
    me_x, me_y, me_z = (lax.axis_index("gx"), lax.axis_index("gy"), lax.axis_index("gz"))

    def at(dx=0, dy=0, dz=0):
        return (
            lax.rem(me_x + (dx + nx), nx) if dx else me_x,
            lax.rem(me_y + (dy + ny), ny) if dy else me_y,
            lax.rem(me_z + (dz + nz), nz) if dz else me_z,
        )

    plane_xy = [(dx, dy) for dx in range(nx) for dy in range(ny) if (dx, dy) != (0, 0)]
    plane_yz = [(dy, dz) for dy in range(ny) for dz in range(nz) if (dy, dz) != (0, 0)]
    edge_dx = (0, 1) if nx == 2 else (-1, 0, 1)
    corners = [(dx, dy, dz) for dz in (1, -1) for dx in edge_dx for dy in (-1, 0, 1)]
    steps = {}
    for dx, dy, dz in (
        [(dx, dy, 0) for dx, dy in SIDES + tuple(plane_xy)]
        + [(0, dy, dz) for dy, dz in plane_yz]
        + corners
    ):
        steps[(dx % nx, dy % ny, dz % nz)] = True
    partners = [at(*step) for step in steps]
    barrier = pltpu.get_barrier_semaphore()
    for partner in partners:
        pl.semaphore_signal(barrier, inc=1, device_id=partner, device_id_type=MESH)
    for fetch in fetches[1:]:
        fetch.start()
    sent = []

    def launch(copies):
        for copy in copies:
            copy.start()
        sent.extend(copies)

    def remote(src, dst, send, recv, device):
        return pltpu.make_async_remote_copy(
            src_ref=src, dst_ref=dst, send_sem=send, recv_sem=recv, device_id=device,
            device_id_type=MESH,
        )

    def span(step, count, first):
        if step == 0:
            return pl.ds(first, count), pl.ds(1, count)
        if step > 0:
            return pl.ds(first + count - 1, 1), pl.ds(0, 1)
        return pl.ds(first, 1), pl.ds(count + 1, 1)

    def side_copies(which, ext, near):
        copies = []
        for at_side, (dx, dy) in enumerate(SIDES):
            if (dx == 0) == near:
                sx, tx = span(dx, CX, 1)
                sy, ty = span(dy, CY, 1)
                copies.append(
                    remote(ext.at[sx, sy], ext.at[tx, ty], xy_send.at[which, at_side],
                           xy_recv.at[which, at_side], at(dx, dy))
                )
        return copies

    lanes = lax.broadcasted_iota(jnp.int32, (C, CZ), 1)
    group = lax.div(lanes, 2)

    def edge_copies(which, near):
        return [
            remote(edge_out.at[which],
                   edge_in.at[which, 0 if dz > 0 else 1, 1 - dx, 1 - dy],
                   z_send.at[which, k], z_recv.at[which, k], at(dx, dy, dz))
            for k, (dx, dy, dz) in enumerate(corners)
            if (dx == 0) == near
        ]

    def exchange(which, ext):
        near = side_copies(which, ext, True) + edge_copies(which, True)
        far = side_copies(which, ext, False) + edge_copies(which, False)
        launch(near + far)
        return near, far

    def pack_edges(which, ext):
        edges = jnp.zeros((C, CZ), jnp.float32)
        for x in range(CX):
            for y in range(CY):
                row = x * CY + y
                rolled = pltpu.roll(ext[x + 1, y + 1].astype(jnp.float32), 1 + 2 * row, 1)
                edges = jnp.where(group == row, rolled, edges)
        edge_out[which] = edges.astype(jnp.bfloat16)

    def build_taps(which, ext, out, p, place_x, x):
        tiles_at = {}
        for y in range(EY):
            place_y, line = (0, CY - 1) if y == 0 else (2, 0) if y == EY - 1 else (1, y - 1)
            if place_y not in tiles_at:
                before, after = (
                    edge_in[which, side, place_x, place_y].astype(jnp.float32) for side in (0, 1)
                )
                tiles_at[place_y] = jnp.where(lanes % 2 == 0, before, after)
            row = x * CY + line
            mid = ext[p, y]
            wide = mid.astype(jnp.float32)
            rim = pltpu.roll(tiles_at[place_y], CZ - 1 - 2 * row, 1)
            low = pltpu.roll(jnp.where(lanes == CZ - 1, rim, wide), 1, 1)
            high = pltpu.roll(jnp.where(lanes == 0, rim, wide), CZ - 1, 1)
            out[p, y, 0:C] = low.astype(jnp.bfloat16)
            out[p, y, C : 2 * C] = mid
            out[p, y, 2 * C : 3 * C] = high.astype(jnp.bfloat16)

    def build_near(which, ext, out):
        def plane(x, carry):
            build_taps(which, ext, out, x + 1, 1, x)
            return carry

        lax.fori_loop(0, CX, plane, 0)

    def build_far(which, ext, out):
        build_taps(which, ext, out, 0, 0, CX - 1)
        build_taps(which, ext, out, CX + 1, 0 if nx == 2 else 2, 0)

    def columns(source, p, y):
        return jnp.concatenate(
            [source[p, pl.ds(y + k, 3)].reshape(9 * C, CZ) for k in range(2)], axis=1
        )

    near_planes, far_planes = range(1, CX + 1), (0, CX + 1)

    def convolve(weights, source, y, planes, results):
        for p in planes:
            taken = [a for a in range(3) if 0 <= p - a < CX]
            product = jnp.dot(weights[taken[0] * C : (taken[-1] + 1) * C, :],
                              columns(source, p, y), preferred_element_type=jnp.float32)
            for k, a in enumerate(taken):
                term = product[k * C : (k + 1) * C]
                results[p - a] = term if results[p - a] is None else results[p - a] + term
        return results

    fetches[0].wait()
    for x in range(CX):
        turned_x = jnp.swapaxes(field[:, x].astype(jnp.float32), 0, 1)
        field_ext[x + 1, 1 : CY + 1] = turned_x.astype(jnp.bfloat16)
    pack_edges(0, field_ext)
    pl.semaphore_wait(barrier, len(partners))
    field_near, field_far = exchange(0, field_ext)
    for fetch in fetches[1:]:
        fetch.wait()

    eye = lax.broadcasted_iota(jnp.int32, (C, C), 0) == lax.broadcasted_iota(jnp.int32, (C, C), 1)

    def to_row(column):
        return jnp.sum(jnp.where(eye, column, 0.0), axis=0, keepdims=True)

    def to_column(row):
        return jnp.sum(jnp.where(eye, row, 0.0), axis=1, keepdims=True)

    lifted = lift_bias[...]
    for k in range(lift_weight.shape[0]):
        lifted = lifted + cosmology[0:1, k : k + 1] * lift_weight[k : k + 1, :]
    hidden = lifted / (1.0 + jnp.exp(-lifted))
    styles_column = (
        jnp.sum(style_t[...] * hidden, axis=1, keepdims=True) + to_column(style_bias[...]) + 1.0
    )
    styles = to_row(styles_column)
    styles_wide = jnp.concatenate([styles] * per, axis=1)
    squares = jnp.zeros((C, CZ), jnp.float32)
    for j in range(tiles):
        members = [
            kernel[per * j + k] if per * j + k < taps else jnp.zeros((C, C), jnp.float32)
            for k in range(per)
        ]
        tile = jnp.concatenate(members, axis=1)
        packed[j] = tile
        modded = tile * styles_wide
        squares = squares + modded * modded
    inv_norm = lax.rsqrt(jnp.sum(squares, axis=1, keepdims=True) + demod_eps)
    turned = []
    for j in range(tiles):
        flat = (packed[j] * styles_wide * inv_norm).T
        turned += [flat[k * C : (k + 1) * C] for k in range(per)]
    turned = turned[:taps][::-1]
    for a in range(3):
        taken = range(9 * a, 9 * a + 9)
        w_fwd[a * C : (a + 1) * C, :] = jnp.concatenate(
            [kernel[t] * styles * inv_norm for t in taken], axis=1
        ).astype(jnp.bfloat16)
        w_bwd[a * C : (a + 1) * C, :] = jnp.concatenate(
            [turned[t] for t in taken], axis=1
        ).astype(jnp.bfloat16)
    offset_column = to_column(offset[...])
    for x in range(CX):
        cot[x] = jnp.swapaxes(cotangent[:, x].astype(jnp.float32), 0, 1)

    for copy in field_near:
        copy.wait_recv()
    build_near(0, field_ext, field_taps)

    depth = taps * C

    edge_x = sorted({0, CX - 1})

    def finish(x, y, sums):
        above = jnp.concatenate([cot[x, y], cot[x, y + 1]], axis=1)
        upstream = (above * silu_slope(sums + offset_column)).astype(jnp.bfloat16)
        up_ext[x + 1, y + 1] = upstream[:, :CZ]
        up_ext[x + 1, y + 2] = upstream[:, CZ:]

    def forward_near(at_pair, carry):
        y = 2 * at_pair
        results = convolve(w_fwd, field_taps, y, near_planes, [None] * CX)
        for x, sums in enumerate(results):
            if x in edge_x:
                held[x, at_pair] = sums
            else:
                finish(x, y, sums)
        return carry

    def forward_far(at_pair, carry):
        y = 2 * at_pair
        results = [held[x, at_pair] if x in edge_x else None for x in range(CX)]
        results = convolve(w_fwd, field_taps, y, far_planes, results)
        for x in edge_x:
            finish(x, y, results[x])
        return carry

    lax.fori_loop(0, CY // 2, forward_near, 0)
    for copy in field_far:
        copy.wait_recv()
    build_far(0, field_ext, field_taps)
    lax.fori_loop(0, CY // 2, forward_far, 0)

    def weigh(at_pair, carry):
        y = 2 * at_pair
        sums, offsets = list(carry[:3]), carry[3]
        ups = []
        for x in range(CX):
            upstream = jnp.concatenate([up_ext[x + 1, y + 1], up_ext[x + 1, y + 2]], axis=1)
            wide = upstream.astype(jnp.float32)
            offsets = offsets + wide[:, :CZ] + wide[:, CZ:]
            ups.append(upstream)
        for p in range(CX + 2):
            taken = [a for a in range(3) if 0 <= p - a < CX]
            product = lax.dot_general(
                jnp.concatenate([ups[p - a] for a in taken], axis=0),
                columns(field_taps, p, y), (((1,), (1,)), ((), ())),
                preferred_element_type=jnp.float32,
            )
            for k, a in enumerate(taken):
                sums[a] = sums[a] + product[k * C : (k + 1) * C]
        return (*sums, offsets)

    *sums, offsets = lax.fori_loop(
        0, CY // 2, weigh,
        (jnp.zeros((C, 9 * C), jnp.float32),) * 3 + (jnp.zeros((C, CZ), jnp.float32),),
    )
    sums = jnp.concatenate(sums, axis=1)
    offset_sum = jnp.sum(offsets, axis=1, keepdims=True)
    for j in range(share.shape[0] // C):
        if (j + 1) * CZ <= depth:
            tile = sums[:, j * CZ : (j + 1) * CZ]
        elif j < tiles:
            used = depth - j * CZ
            tile = jnp.concatenate(
                [sums[:, j * CZ : depth], jnp.broadcast_to(offset_sum, (C, CZ - used))], axis=1
            )
        else:
            tile = jnp.zeros((C, CZ), jnp.float32)
        share[j * C : (j + 1) * C] = tile.astype(jnp.bfloat16)

    rows_z = share.shape[0] // nz
    rows_y = rows_z // ny

    def rows_at(base, count):
        return pl.ds(pl.multiple_of(base, 16), count)

    reduce_z = []
    for k in range(1, nz):
        there = at(dz=k)
        reduce_z.append(remote(share.at[rows_at(there[2] * rows_z, rows_z)], from_z.at[k - 1],
                               rz_send.at[k - 1], rz_recv.at[k - 1], there))
    launch(reduce_z)

    pack_edges(1, up_ext)
    up_near, up_far = exchange(1, up_ext)

    for copy in reduce_z:
        copy.wait_recv()
    mine = share[rows_at(me_z * rows_z, rows_z), :].astype(jnp.float32)
    for k in range(1, nz):
        mine = mine + from_z[k - 1].astype(jnp.float32)
    part_z[...] = mine.astype(jnp.bfloat16)
    my_slot = me_x * ny + me_y
    reduce_xy = []
    for k, (dx, dy) in enumerate(plane_xy):
        there = at(dx, dy)
        reduce_xy.append(remote(part_z.at[rows_at(there[1] * rows_y, rows_y)], from_xy.at[my_slot],
                                rxy_send.at[k], rxy_recv.at[k], there))
    launch(reduce_xy)
    from_xy[my_slot] = part_z[rows_at(me_y * rows_y, rows_y), :]

    for copy in up_near:
        copy.wait_recv()
    build_near(1, up_ext, up_taps)

    def backward_near(at_pair, carry):
        y = 2 * at_pair
        for x, sums in enumerate(convolve(w_bwd, up_taps, y, near_planes, [None] * CX)):
            held[x, at_pair] = sums
        return carry

    def backward_far(at_pair, carry):
        y = 2 * at_pair
        results = [held[x, at_pair] for x in range(CX)]
        for x, sums in enumerate(convolve(w_bwd, up_taps, y, far_planes, results)):
            turned_back[x, y] = sums[:, :CZ]
            turned_back[x, y + 1] = sums[:, CZ:]
        return carry

    lax.fori_loop(0, CY // 2, backward_near, 0)

    for copy in reduce_xy:
        copy.wait_recv()
    mine = from_xy[0].astype(jnp.float32)
    for k in range(1, nx * ny):
        mine = mine + from_xy[k].astype(jnp.float32)
    own = rows_at(me_z * rows_z + me_y * rows_y, rows_y)
    total[own, :] = mine.astype(jnp.bfloat16)
    gather = [
        remote(total.at[own], total.at[own], g_send.at[k], g_recv.at[k], at(0, dy, dz))
        for k, (dy, dz) in enumerate(plane_yz)
    ]
    launch(gather)
    for copy in up_far:
        copy.wait_recv()
    build_far(1, up_ext, up_taps)
    lax.fori_loop(0, CY // 2, backward_far, 0)
    for x in range(CX):
        grad[:, x] = jnp.swapaxes(turned_back[x], 0, 1).astype(jnp.bfloat16)
    for copy in gather:
        copy.wait_recv()

    last = taps - per * (tiles - 1)
    projected = jnp.zeros((C, CZ), jnp.float32)
    sum_tiles, modded_tiles = [], []
    for j in range(tiles):
        tile = total[j * C : (j + 1) * C, :].astype(jnp.float32)
        if j == tiles - 1:
            offset_row = to_row(tile[:, last * C : last * C + 1])
            tile = jnp.where(lanes < last * C, tile, 0.0)
        modded = packed[j] * styles_wide
        projected = projected + tile * modded
        sum_tiles.append(tile)
        modded_tiles.append(modded)
    projected = jnp.sum(projected, axis=1, keepdims=True)
    scale = inv_norm * inv_norm * projected
    raws = []
    square = jnp.zeros((C, CZ), jnp.float32)
    along = jnp.zeros((C, CZ), jnp.float32)
    for j in range(tiles):
        mod_grad = inv_norm * (sum_tiles[j] - modded_tiles[j] * scale)
        raw = mod_grad * styles_wide
        along = along + mod_grad * packed[j]
        square = square + raw * raw
        raws.append(raw)
    along = jnp.sum(along, axis=0, keepdims=True)
    styles_grad = along[:, 0:C]
    for k in range(1, per):
        styles_grad = styles_grad + along[:, k * C : (k + 1) * C]
    styles_grad_column = to_column(styles_grad)
    hidden_grad = jnp.sum(style_t[...] * styles_grad_column, axis=0, keepdims=True)
    lifted_grad = hidden_grad * silu_slope(lifted)
    style_raw = styles_grad_column * hidden
    lift_raws = [
        cosmology[0:1, k : k + 1] * lifted_grad for k in range(lift_weight.shape[0])
    ]

    def sum_all(values):
        return jnp.sum(jnp.sum(values, axis=1, keepdims=True), axis=0, keepdims=True)

    square_sum = sum_all(square)
    for member in [offset_row, lifted_grad, style_raw, styles_grad] + lift_raws:
        square_sum = square_sum + sum_all(member * member)
    entries = taps * C * C + 2 * C + (1 + lift_weight.shape[0] + C) * lifted.shape[1]
    factor = jnp.minimum(1.0, lax.rsqrt(square_sum / entries + clip_eps))
    for j in range(tiles):
        grad_packed[j] = raws[j] * factor
    for copy in sent:
        copy.wait_send()
    grad_style_t[...] = style_raw * factor
    wide = lifted.shape[1]
    small = jnp.concatenate([offset_row, styles_grad], axis=1)
    grad_rows[0:1, 0 : 2 * C] = small * factor
    grad_rows[1:2, :] = lifted_grad * factor
    for k in range(lift_weight.shape[0]):
        grad_rows[k + 2 : k + 3, :] = lift_raws[k] * factor


def hand_out(
    grad_in, grad_packed, grad_rows, grad_style_in,
    grad, grad_kernel, grad_offset, grad_lift, grad_liftbias, grad_style_t, grad_stylebias,
):
    C = grad_packed.shape[1]
    per = grad_packed.shape[2] // C
    grad[...] = grad_in[...]
    for t in range(grad_kernel.shape[0]):
        k = t % per
        grad_kernel[t] = grad_packed[t // per][:, k * C : (k + 1) * C]
    grad_offset[...] = grad_rows[0:1, 0:C]
    grad_stylebias[...] = grad_rows[0:1, C : 2 * C]
    grad_liftbias[...] = grad_rows[1:2, :]
    grad_lift[...] = grad_rows[2 : 2 + grad_lift.shape[0], :]
    grad_style_t[...] = grad_style_in[...]


def body(
    sizes, field, cotangent, cosmology, lift_weight, lift_bias, style_weight, style_bias, kernel,
    offset,
):
    nx, ny, nz = sizes
    C, CX, CY, CZ = field.shape
    HID = lift_bias.shape[0]
    taps = kernel.shape[2] * kernel.shape[3] * kernel.shape[4]
    per = CZ // C
    tiles = (taps + per) // per
    unit = nz * ny * 16
    rows = -(-tiles * C // unit) * unit
    f32, bf16 = jnp.float32, jnp.bfloat16
    dma = pltpu.SemaphoreType.DMA
    vmem = pl.BlockSpec(memory_space=pltpu.VMEM)
    results = pl.pallas_call(
        functools.partial(kernel_body, sizes),
        out_shape=[
            jax.ShapeDtypeStruct(field.shape, bf16),
            jax.ShapeDtypeStruct((tiles, C, CZ), f32),
            jax.ShapeDtypeStruct((8, HID), f32),
            jax.ShapeDtypeStruct((C, HID), f32),
        ],
        in_specs=[pl.BlockSpec(memory_space=pltpu.HBM)] * 9,
        out_specs=[vmem] * 4,
        scratch_shapes=[
            pltpu.VMEM(field.shape, bf16),
            pltpu.VMEM(field.shape, bf16),
            pltpu.VMEM((1, cosmology.shape[0]), f32),
            pltpu.VMEM(lift_weight.shape, f32),
            pltpu.VMEM((1, HID), f32),
            pltpu.VMEM((C, HID), f32),
            pltpu.VMEM((1, C), f32),
            pltpu.VMEM((taps, C, C), f32),
            pltpu.VMEM((1, C), f32),
            dma((9,)),
            pltpu.VMEM((CX + 2, CY + 2, C, CZ), bf16),
            pltpu.VMEM((CX + 2, CY + 2, C, CZ), bf16),
            pltpu.VMEM((CX + 2, CY + 2, 3 * C, CZ), bf16),
            pltpu.VMEM((CX + 2, CY + 2, 3 * C, CZ), bf16),
            pltpu.VMEM((2, C, CZ), bf16),
            pltpu.VMEM((2, 2, 3, 3, C, CZ), bf16),
            pltpu.VMEM((3 * C, 9 * C), bf16),
            pltpu.VMEM((3 * C, 9 * C), bf16),
            pltpu.VMEM((tiles, C, CZ), f32),
            pltpu.VMEM((CX, CY, C, CZ), f32),
            pltpu.VMEM((CX, CY, C, CZ), f32),
            pltpu.VMEM((CX, CY // 2, C, 2 * CZ), f32),
            pltpu.VMEM((rows, CZ), bf16),
            pltpu.VMEM((nz - 1, rows // nz, CZ), bf16),
            pltpu.VMEM((rows // nz, CZ), bf16),
            pltpu.VMEM((nx * ny, rows // nz // ny, CZ), bf16),
            pltpu.VMEM((rows, CZ), bf16),
            dma((2, 8)), dma((2, 8)), dma((2, 18)), dma((2, 18)),
            dma((nz - 1,)), dma((nz - 1,)), dma((nx * ny - 1,)), dma((nx * ny - 1,)),
            dma((ny * nz - 1,)), dma((ny * nz - 1,)),
        ],
        compiler_params=pltpu.CompilerParams(
            collective_id=0, has_side_effects=True, vmem_limit_bytes=60 * 1024 * 1024
        ),
    )(
        field,
        cotangent,
        cosmology[None],
        lift_weight,
        lift_bias[None],
        style_weight.T,
        style_bias[None],
        jnp.transpose(kernel, (2, 3, 4, 0, 1)).reshape(taps, C, C),
        offset[None],
    )
    grad, grad_kernel, grad_offset, grad_lift, grad_liftbias, grad_style_t, grad_stylebias = (
        pl.pallas_call(
            hand_out,
            out_shape=[
                jax.ShapeDtypeStruct(field.shape, bf16),
                jax.ShapeDtypeStruct((taps, C, C), f32),
                jax.ShapeDtypeStruct((1, C), f32),
                jax.ShapeDtypeStruct(lift_weight.shape, f32),
                jax.ShapeDtypeStruct((1, HID), f32),
                jax.ShapeDtypeStruct((C, HID), f32),
                jax.ShapeDtypeStruct((1, C), f32),
            ],
            in_specs=[vmem] * 4,
            out_specs=[vmem] * 7,
            compiler_params=pltpu.CompilerParams(vmem_limit_bytes=60 * 1024 * 1024),
        )(*results)
    )
    return (
        grad,
        jnp.transpose(grad_kernel.reshape(kernel.shape[2:] + (C, C)), (3, 4, 0, 1, 2)),
        grad_offset[0],
        grad_lift,
        grad_liftbias[0],
        grad_style_t.T,
        grad_stylebias[0],
    )


def solution(mesh):
    sizes = (mesh.shape["gx"], mesh.shape["gy"], mesh.shape["gz"])
    placed = P(None, "gx", "gy", "gz")
    return jax.shard_map(
        functools.partial(body, sizes),
        mesh=mesh,
        in_specs=(placed, placed, P(), P(), P(), P(), P(), P(), P()),
        out_specs=(placed, P(), P(), P(), P(), P(), P()),
        check_vma=False,
    )
```

```python
import functools

import jax
import jax.numpy as jnp
from jax import lax
from jax.experimental import pallas as pl
from jax.experimental.pallas import tpu as pltpu
from jax.sharding import PartitionSpec as P

demod_eps = 1e-06
clip_eps = 1e-06
MESH = pl.DeviceIdType.MESH
SIDES = tuple((dx, dy) for dx in (-1, 0, 1) for dy in (-1, 0, 1) if (dx, dy) != (0, 0))


def silu_slope(values):
    logistic = 1.0 / (1.0 + jnp.exp(-values))
    return logistic * (1.0 + values * (1.0 - logistic))


def kernel_body(
    sizes,
    field_hbm, cotangent_hbm, cosmology_hbm, lift_weight_hbm, lift_bias_hbm, style_hbm,
    style_bias_hbm, kernel_hbm, offset_hbm,
    grad, grad_packed, grad_rows, grad_style_t,
    field, cotangent, cosmology, lift_weight, lift_bias, style_t, style_bias, kernel, offset,
    fetch_sem, field_ext, up_ext, field_taps, up_taps, edge_out, edge_in, w_fwd, w_bwd, packed, field_rows, cot, turned_back, held, up_turned,
    share, from_z, part_z, from_xy, total,
    xy_send, xy_recv, z_send, z_recv, rz_send, rz_recv, rxy_send, rxy_recv, g_send, g_recv,
):
    nx, ny, nz = sizes
    C, CX, CY, CZ = field.shape
    EY = CY + 2
    taps = kernel.shape[0]
    per = CZ // C
    tiles = (taps + per) // per
    fetches = [
        pltpu.make_async_copy(source, there, fetch_sem.at[k])
        for k, (source, there) in enumerate(
            zip(
                (field_hbm, kernel_hbm, cosmology_hbm, lift_weight_hbm, lift_bias_hbm, style_hbm,
                 style_bias_hbm, offset_hbm, cotangent_hbm),
                (field, kernel, cosmology, lift_weight, lift_bias, style_t, style_bias, offset,
                 cotangent),
            )
        )
    ]
    fetches[0].start()
    me_x, me_y, me_z = (lax.axis_index("gx"), lax.axis_index("gy"), lax.axis_index("gz"))

    def at(dx=0, dy=0, dz=0):
        return (
            lax.rem(me_x + (dx + nx), nx) if dx else me_x,
            lax.rem(me_y + (dy + ny), ny) if dy else me_y,
            lax.rem(me_z + (dz + nz), nz) if dz else me_z,
        )

    plane_xy = [(dx, dy) for dx in range(nx) for dy in range(ny) if (dx, dy) != (0, 0)]
    plane_yz = [(dy, dz) for dy in range(ny) for dz in range(nz) if (dy, dz) != (0, 0)]
    edge_dx = (0, 1) if nx == 2 else (-1, 0, 1)
    corners = [(dx, dy, dz) for dz in (1, -1) for dx in edge_dx for dy in (-1, 0, 1)]
    steps = {}
    for dx, dy, dz in (
        [(dx, dy, 0) for dx, dy in SIDES + tuple(plane_xy)]
        + [(0, dy, dz) for dy, dz in plane_yz]
        + corners
    ):
        steps[(dx % nx, dy % ny, dz % nz)] = True
    partners = [at(*step) for step in steps]
    barrier = pltpu.get_barrier_semaphore()
    for partner in partners:
        pl.semaphore_signal(barrier, inc=1, device_id=partner, device_id_type=MESH)
    for fetch in fetches[1:]:
        fetch.start()
    sent = []

    def launch(copies):
        for copy in copies:
            copy.start()
        sent.extend(copies)

    def remote(src, dst, send, recv, device):
        return pltpu.make_async_remote_copy(
            src_ref=src, dst_ref=dst, send_sem=send, recv_sem=recv, device_id=device,
            device_id_type=MESH,
        )

    def span(step, count, first):
        if step == 0:
            return pl.ds(first, count), pl.ds(1, count)
        if step > 0:
            return pl.ds(first + count - 1, 1), pl.ds(0, 1)
        return pl.ds(first, 1), pl.ds(count + 1, 1)

    def side_copies(which, ext, near):
        copies = []
        for at_side, (dx, dy) in enumerate(SIDES):
            if (dx == 0) == near:
                sx, tx = span(dx, CX, 1)
                sy, ty = span(dy, CY, 1)
                copies.append(
                    remote(ext.at[sx, sy], ext.at[tx, ty], xy_send.at[which, at_side],
                           xy_recv.at[which, at_side], at(dx, dy))
                )
        return copies

    lanes = lax.broadcasted_iota(jnp.int32, (C, CZ), 1)
    group = lax.div(lanes, 2)

    def edge_copies(which, near):
        return [
            remote(edge_out.at[which],
                   edge_in.at[which, 0 if dz > 0 else 1, 1 - dx, 1 - dy],
                   z_send.at[which, k], z_recv.at[which, k], at(dx, dy, dz))
            for k, (dx, dy, dz) in enumerate(corners)
            if (dx == 0) == near
        ]

    def exchange(which, ext):
        near = side_copies(which, ext, True) + edge_copies(which, True)
        far = side_copies(which, ext, False) + edge_copies(which, False)
        launch(near + far)
        return near, far

    def pack_edges(which, ext):
        edges = jnp.zeros((C, CZ), jnp.float32)
        for x in range(CX):
            for y in range(CY):
                row = x * CY + y
                rolled = pltpu.roll(ext[x + 1, y + 1].astype(jnp.float32), 1 + 2 * row, 1)
                edges = jnp.where(group == row, rolled, edges)
        edge_out[which] = edges.astype(jnp.bfloat16)

    def build_taps(which, ext, out, p, place_x, x):
        tiles_at = {}
        for y in range(EY):
            place_y, source_y = (0, CY - 1) if y == 0 else (2, 0) if y == EY - 1 else (1, y - 1)
            if place_y not in tiles_at:
                before, after = (
                    edge_in[which, side, place_x, place_y].astype(jnp.float32) for side in (0, 1)
                )
                tiles_at[place_y] = jnp.where(lanes % 2 == 0, before, after)
            row = x * CY + source_y
            mid = ext[p, y]
            wide = mid.astype(jnp.float32)
            rim = pltpu.roll(tiles_at[place_y], CZ - 1 - 2 * row, 1)
            low = pltpu.roll(jnp.where(lanes == CZ - 1, rim, wide), 1, 1)
            high = pltpu.roll(jnp.where(lanes == 0, rim, wide), CZ - 1, 1)
            out[p, y, 0:C] = low.astype(jnp.bfloat16)
            out[p, y, C : 2 * C] = mid
            out[p, y, 2 * C : 3 * C] = high.astype(jnp.bfloat16)

    def build_near(which, ext, out):
        def plane(x, carry):
            build_taps(which, ext, out, x + 1, 1, x)
            return carry

        lax.fori_loop(0, CX, plane, 0)

    def build_far(which, ext, out):
        build_taps(which, ext, out, 0, 0, CX - 1)
        build_taps(which, ext, out, CX + 1, 0 if nx == 2 else 2, 0)

    def columns(source, p, y):
        return jnp.concatenate(
            [source[p, pl.ds(y + k, 3)].reshape(9 * C, CZ) for k in range(2)], axis=1
        )

    near_planes, far_planes = range(1, CX + 1), (0, CX + 1)

    def convolve(weights, source, y, planes, results):
        for p in planes:
            taken = [a for a in range(3) if 0 <= p - a < CX]
            product = jnp.dot(weights[taken[0] * C : (taken[-1] + 1) * C, :],
                              columns(source, p, y), preferred_element_type=jnp.float32)
            for k, a in enumerate(taken):
                term = product[k * C : (k + 1) * C]
                results[p - a] = term if results[p - a] is None else results[p - a] + term
        return results

    def line(x, y):
        return pl.ds(x * CY + y, C, stride=CX * CY)

    fetches[0].wait()
    field_rows[...] = field[...].astype(jnp.float32).reshape(C * CX * CY, CZ)
    for x in range(CX):
        for y in range(CY):
            field_ext[x + 1, y + 1] = field_rows[line(x, y), :].astype(jnp.bfloat16)
    pack_edges(0, field_ext)
    pl.semaphore_wait(barrier, len(partners))
    field_near, field_far = exchange(0, field_ext)
    for fetch in fetches[1:]:
        fetch.wait()

    eye = lax.broadcasted_iota(jnp.int32, (C, C), 0) == lax.broadcasted_iota(jnp.int32, (C, C), 1)

    def to_row(column):
        return jnp.sum(jnp.where(eye, column, 0.0), axis=0, keepdims=True)

    def to_column(row):
        return jnp.sum(jnp.where(eye, row, 0.0), axis=1, keepdims=True)

    lifted = lift_bias[...]
    for k in range(lift_weight.shape[0]):
        lifted = lifted + cosmology[0:1, k : k + 1] * lift_weight[k : k + 1, :]
    hidden = lifted / (1.0 + jnp.exp(-lifted))
    styles_column = (
        jnp.sum(style_t[...] * hidden, axis=1, keepdims=True) + to_column(style_bias[...]) + 1.0
    )
    styles = to_row(styles_column)
    styles_wide = jnp.concatenate([styles] * per, axis=1)
    squares = jnp.zeros((C, CZ), jnp.float32)
    for j in range(tiles):
        members = [
            kernel[per * j + k] if per * j + k < taps else jnp.zeros((C, C), jnp.float32)
            for k in range(per)
        ]
        tile = jnp.concatenate(members, axis=1)
        packed[j] = tile
        modded = tile * styles_wide
        squares = squares + modded * modded
    inv_norm = lax.rsqrt(jnp.sum(squares, axis=1, keepdims=True) + demod_eps)
    turned = []
    for j in range(tiles):
        flat = (packed[j] * styles_wide * inv_norm).T
        turned += [flat[k * C : (k + 1) * C] for k in range(per)]
    turned = turned[:taps][::-1]
    for a in range(3):
        taken = range(9 * a, 9 * a + 9)
        w_fwd[a * C : (a + 1) * C, :] = jnp.concatenate(
            [kernel[t] * styles * inv_norm for t in taken], axis=1
        ).astype(jnp.bfloat16)
        w_bwd[a * C : (a + 1) * C, :] = jnp.concatenate(
            [turned[t] for t in taken], axis=1
        ).astype(jnp.bfloat16)
    offset_column = to_column(offset[...])
    cot[...] = cotangent[...].astype(jnp.float32).reshape(C * CX * CY, CZ)

    for copy in field_near:
        copy.wait_recv()
    build_near(0, field_ext, field_taps)

    depth = taps * C

    edge_x = sorted({0, CX - 1})

    def finish(x, y, sums):
        above = jnp.concatenate([cot[line(x, y), :], cot[line(x, y + 1), :]], axis=1)
        upstream = (above * silu_slope(sums + offset_column)).astype(jnp.bfloat16)
        up_ext[x + 1, y + 1] = upstream[:, :CZ]
        up_ext[x + 1, y + 2] = upstream[:, CZ:]

    def forward_near(at_pair, carry):
        y = 2 * at_pair
        results = convolve(w_fwd, field_taps, y, near_planes, [None] * CX)
        for x, sums in enumerate(results):
            if x in edge_x:
                held[x, at_pair] = sums
            else:
                finish(x, y, sums)
        return carry

    def forward_far(at_pair, carry):
        y = 2 * at_pair
        results = [held[x, at_pair] if x in edge_x else None for x in range(CX)]
        results = convolve(w_fwd, field_taps, y, far_planes, results)
        for x in edge_x:
            finish(x, y, results[x])
        return carry

    lax.fori_loop(0, CY // 2, forward_near, 0)
    for copy in field_far:
        copy.wait_recv()
    build_far(0, field_ext, field_taps)
    lax.fori_loop(0, CY // 2, forward_far, 0)

    offsets = jnp.zeros((C, CZ), jnp.float32)
    blank = [jnp.zeros((C, CZ), jnp.float32)] * (per - CX)
    for y in range(CY):
        ups = [up_ext[x + 1, y + 1].astype(jnp.float32) for x in range(CX)]
        for up in ups:
            offsets = offsets + up
        up_turned[y * CZ : (y + 1) * CZ, :] = jnp.concatenate(ups + blank, axis=0).T.astype(
            jnp.bfloat16
        )
    block = lax.div(lax.broadcasted_iota(jnp.int32, (9 * C, CZ), 1), C)
    products = []
    for p in range(CX + 2):
        streamed = jnp.concatenate(
            [field_taps[p, y : y + 3].reshape(9 * C, CZ) for y in range(CY)], axis=1
        )
        products.append(jnp.dot(streamed, up_turned[...], preferred_element_type=jnp.float32))
    merged = jnp.zeros((9 * C, CZ), jnp.float32)
    for a in range(3):
        chosen = products[a]
        for x in range(1, CX):
            chosen = jnp.where(block == x, products[a + x], chosen)
        shift = CZ // 2
        while shift >= C:
            chosen = chosen + pltpu.roll(chosen, shift, 1)
            shift //= 2
        merged = jnp.where(block == a, chosen, merged)
    flats = [merged[k : min(k + CZ, 9 * C)].T for k in range(0, 9 * C, CZ)]
    sums = jnp.concatenate(
        [flat[a * C : (a + 1) * C] for a in range(3) for flat in flats], axis=1
    )
    offset_sum = jnp.sum(offsets, axis=1, keepdims=True)
    for j in range(share.shape[0] // C):
        if (j + 1) * CZ <= depth:
            tile = sums[:, j * CZ : (j + 1) * CZ]
        elif j < tiles:
            used = depth - j * CZ
            tile = jnp.concatenate(
                [sums[:, j * CZ : depth], jnp.broadcast_to(offset_sum, (C, CZ - used))], axis=1
            )
        else:
            tile = jnp.zeros((C, CZ), jnp.float32)
        share[j * C : (j + 1) * C] = tile.astype(jnp.bfloat16)

    rows_z = share.shape[0] // nz
    rows_y = rows_z // ny

    def rows_at(base, count):
        return pl.ds(pl.multiple_of(base, 16), count)

    reduce_z = []
    for k in range(1, nz):
        there = at(dz=k)
        reduce_z.append(remote(share.at[rows_at(there[2] * rows_z, rows_z)], from_z.at[k - 1],
                               rz_send.at[k - 1], rz_recv.at[k - 1], there))
    launch(reduce_z)

    pack_edges(1, up_ext)
    up_near, up_far = exchange(1, up_ext)

    for copy in reduce_z:
        copy.wait_recv()
    mine = share[rows_at(me_z * rows_z, rows_z), :].astype(jnp.float32)
    for k in range(1, nz):
        mine = mine + from_z[k - 1].astype(jnp.float32)
    part_z[...] = mine.astype(jnp.bfloat16)
    my_slot = me_x * ny + me_y
    reduce_xy = []
    for k, (dx, dy) in enumerate(plane_xy):
        there = at(dx, dy)
        reduce_xy.append(remote(part_z.at[rows_at(there[1] * rows_y, rows_y)], from_xy.at[my_slot],
                                rxy_send.at[k], rxy_recv.at[k], there))
    launch(reduce_xy)
    from_xy[my_slot] = part_z[rows_at(me_y * rows_y, rows_y), :]

    for copy in up_near:
        copy.wait_recv()
    build_near(1, up_ext, up_taps)

    def backward_near(at_pair, carry):
        y = 2 * at_pair
        for x, sums in enumerate(convolve(w_bwd, up_taps, y, near_planes, [None] * CX)):
            held[x, at_pair] = sums
        return carry

    def backward_far(at_pair, carry):
        y = 2 * at_pair
        results = [held[x, at_pair] for x in range(CX)]
        for x, sums in enumerate(convolve(w_bwd, up_taps, y, far_planes, results)):
            turned_back[line(x, y), :] = sums[:, :CZ]
            turned_back[line(x, y + 1), :] = sums[:, CZ:]
        return carry

    lax.fori_loop(0, CY // 2, backward_near, 0)

    for copy in reduce_xy:
        copy.wait_recv()
    mine = from_xy[0].astype(jnp.float32)
    for k in range(1, nx * ny):
        mine = mine + from_xy[k].astype(jnp.float32)
    own = rows_at(me_z * rows_z + me_y * rows_y, rows_y)
    total[own, :] = mine.astype(jnp.bfloat16)
    gather = [
        remote(total.at[own], total.at[own], g_send.at[k], g_recv.at[k], at(0, dy, dz))
        for k, (dy, dz) in enumerate(plane_yz)
    ]
    launch(gather)
    for copy in up_far:
        copy.wait_recv()
    build_far(1, up_ext, up_taps)
    lax.fori_loop(0, CY // 2, backward_far, 0)
    grad[...] = turned_back[...].reshape(grad.shape).astype(jnp.bfloat16)
    for copy in gather:
        copy.wait_recv()

    last = taps - per * (tiles - 1)
    projected = jnp.zeros((C, CZ), jnp.float32)
    sum_tiles, modded_tiles = [], []
    for j in range(tiles):
        tile = total[j * C : (j + 1) * C, :].astype(jnp.float32)
        if j == tiles - 1:
            offset_row = to_row(tile[:, last * C : last * C + 1])
            tile = jnp.where(lanes < last * C, tile, 0.0)
        modded = packed[j] * styles_wide
        projected = projected + tile * modded
        sum_tiles.append(tile)
        modded_tiles.append(modded)
    projected = jnp.sum(projected, axis=1, keepdims=True)
    scale = inv_norm * inv_norm * projected
    raws = []
    square = jnp.zeros((C, CZ), jnp.float32)
    along = jnp.zeros((C, CZ), jnp.float32)
    for j in range(tiles):
        mod_grad = inv_norm * (sum_tiles[j] - modded_tiles[j] * scale)
        raw = mod_grad * styles_wide
        along = along + mod_grad * packed[j]
        square = square + raw * raw
        raws.append(raw)
    along = jnp.sum(along, axis=0, keepdims=True)
    styles_grad = along[:, 0:C]
    for k in range(1, per):
        styles_grad = styles_grad + along[:, k * C : (k + 1) * C]
    styles_grad_column = to_column(styles_grad)
    hidden_grad = jnp.sum(style_t[...] * styles_grad_column, axis=0, keepdims=True)
    lifted_grad = hidden_grad * silu_slope(lifted)
    style_raw = styles_grad_column * hidden
    lift_raws = [
        cosmology[0:1, k : k + 1] * lifted_grad for k in range(lift_weight.shape[0])
    ]

    def sum_all(values):
        return jnp.sum(jnp.sum(values, axis=1, keepdims=True), axis=0, keepdims=True)

    square_sum = sum_all(square)
    for member in [offset_row, lifted_grad, style_raw, styles_grad] + lift_raws:
        square_sum = square_sum + sum_all(member * member)
    entries = taps * C * C + 2 * C + (1 + lift_weight.shape[0] + C) * lifted.shape[1]
    factor = jnp.minimum(1.0, lax.rsqrt(square_sum / entries + clip_eps))
    for j in range(tiles):
        grad_packed[j] = raws[j] * factor
    for copy in sent:
        copy.wait_send()
    grad_style_t[...] = style_raw * factor
    wide = lifted.shape[1]
    small = jnp.concatenate([offset_row, styles_grad], axis=1)
    grad_rows[0:1, 0 : 2 * C] = small * factor
    grad_rows[1:2, :] = lifted_grad * factor
    for k in range(lift_weight.shape[0]):
        grad_rows[k + 2 : k + 3, :] = lift_raws[k] * factor


def hand_out(
    grad_in, grad_packed, grad_rows, grad_style_in,
    grad, grad_kernel, grad_offset, grad_lift, grad_liftbias, grad_style_t, grad_stylebias,
):
    C = grad_packed.shape[1]
    per = grad_packed.shape[2] // C
    grad[...] = grad_in[...]
    for t in range(grad_kernel.shape[0]):
        k = t % per
        grad_kernel[t] = grad_packed[t // per][:, k * C : (k + 1) * C]
    grad_offset[...] = grad_rows[0:1, 0:C]
    grad_stylebias[...] = grad_rows[0:1, C : 2 * C]
    grad_liftbias[...] = grad_rows[1:2, :]
    grad_lift[...] = grad_rows[2 : 2 + grad_lift.shape[0], :]
    grad_style_t[...] = grad_style_in[...]


def body(
    sizes, field, cotangent, cosmology, lift_weight, lift_bias, style_weight, style_bias, kernel,
    offset,
):
    nx, ny, nz = sizes
    C, CX, CY, CZ = field.shape
    HID = lift_bias.shape[0]
    taps = kernel.shape[2] * kernel.shape[3] * kernel.shape[4]
    per = CZ // C
    tiles = (taps + per) // per
    unit = nz * ny * 16
    rows = -(-tiles * C // unit) * unit
    f32, bf16 = jnp.float32, jnp.bfloat16
    dma = pltpu.SemaphoreType.DMA
    vmem = pl.BlockSpec(memory_space=pltpu.VMEM)
    results = pl.pallas_call(
        functools.partial(kernel_body, sizes),
        out_shape=[
            jax.ShapeDtypeStruct(field.shape, bf16),
            jax.ShapeDtypeStruct((tiles, C, CZ), f32),
            jax.ShapeDtypeStruct((8, HID), f32),
            jax.ShapeDtypeStruct((C, HID), f32),
        ],
        in_specs=[pl.BlockSpec(memory_space=pltpu.HBM)] * 9,
        out_specs=[vmem] * 4,
        scratch_shapes=[
            pltpu.VMEM(field.shape, bf16),
            pltpu.VMEM(field.shape, bf16),
            pltpu.VMEM((1, cosmology.shape[0]), f32),
            pltpu.VMEM(lift_weight.shape, f32),
            pltpu.VMEM((1, HID), f32),
            pltpu.VMEM((C, HID), f32),
            pltpu.VMEM((1, C), f32),
            pltpu.VMEM((taps, C, C), f32),
            pltpu.VMEM((1, C), f32),
            dma((9,)),
            pltpu.VMEM((CX + 2, CY + 2, C, CZ), bf16),
            pltpu.VMEM((CX + 2, CY + 2, C, CZ), bf16),
            pltpu.VMEM((CX + 2, CY + 2, 3 * C, CZ), bf16),
            pltpu.VMEM((CX + 2, CY + 2, 3 * C, CZ), bf16),
            pltpu.VMEM((2, C, CZ), bf16),
            pltpu.VMEM((2, 2, 3, 3, C, CZ), bf16),
            pltpu.VMEM((3 * C, 9 * C), bf16),
            pltpu.VMEM((3 * C, 9 * C), bf16),
            pltpu.VMEM((tiles, C, CZ), f32),
            pltpu.VMEM((C * CX * CY, CZ), f32),
            pltpu.VMEM((C * CX * CY, CZ), f32),
            pltpu.VMEM((C * CX * CY, CZ), f32),
            pltpu.VMEM((CX, CY // 2, C, 2 * CZ), f32),
            pltpu.VMEM((CY * CZ, CZ), bf16),
            pltpu.VMEM((rows, CZ), bf16),
            pltpu.VMEM((nz - 1, rows // nz, CZ), bf16),
            pltpu.VMEM((rows // nz, CZ), bf16),
            pltpu.VMEM((nx * ny, rows // nz // ny, CZ), bf16),
            pltpu.VMEM((rows, CZ), bf16),
            dma((2, 8)), dma((2, 8)), dma((2, 18)), dma((2, 18)),
            dma((nz - 1,)), dma((nz - 1,)), dma((nx * ny - 1,)), dma((nx * ny - 1,)),
            dma((ny * nz - 1,)), dma((ny * nz - 1,)),
        ],
        compiler_params=pltpu.CompilerParams(
            collective_id=0, has_side_effects=True, vmem_limit_bytes=60 * 1024 * 1024
        ),
    )(
        field,
        cotangent,
        cosmology[None],
        lift_weight,
        lift_bias[None],
        style_weight.T,
        style_bias[None],
        jnp.transpose(kernel, (2, 3, 4, 0, 1)).reshape(taps, C, C),
        offset[None],
    )
    grad, grad_kernel, grad_offset, grad_lift, grad_liftbias, grad_style_t, grad_stylebias = (
        pl.pallas_call(
            hand_out,
            out_shape=[
                jax.ShapeDtypeStruct(field.shape, bf16),
                jax.ShapeDtypeStruct((taps, C, C), f32),
                jax.ShapeDtypeStruct((1, C), f32),
                jax.ShapeDtypeStruct(lift_weight.shape, f32),
                jax.ShapeDtypeStruct((1, HID), f32),
                jax.ShapeDtypeStruct((C, HID), f32),
                jax.ShapeDtypeStruct((1, C), f32),
            ],
            in_specs=[vmem] * 4,
            out_specs=[vmem] * 7,
            compiler_params=pltpu.CompilerParams(vmem_limit_bytes=60 * 1024 * 1024),
        )(*results)
    )
    return (
        grad,
        jnp.transpose(grad_kernel.reshape(kernel.shape[2:] + (C, C)), (3, 4, 0, 1, 2)),
        grad_offset[0],
        grad_lift,
        grad_liftbias[0],
        grad_style_t.T,
        grad_stylebias[0],
    )


def solution(mesh):
    sizes = (mesh.shape["gx"], mesh.shape["gy"], mesh.shape["gz"])
    placed = P(None, "gx", "gy", "gz")
    return jax.shard_map(
        functools.partial(body, sizes),
        mesh=mesh,
        in_specs=(placed, placed, P(), P(), P(), P(), P(), P(), P()),
        out_specs=(placed, P(), P(), P(), P(), P(), P()),
        check_vma=False,
    )
```

```python
import functools

import jax
import jax.numpy as jnp
from jax import lax
from jax.experimental import pallas as pl
from jax.experimental.pallas import tpu as pltpu
from jax.sharding import PartitionSpec as P

demod_eps = 1e-06
clip_eps = 1e-06
MESH = pl.DeviceIdType.MESH
SIDES = tuple((dx, dy) for dx in (-1, 0, 1) for dy in (-1, 0, 1) if (dx, dy) != (0, 0))


def silu_slope(values):
    logistic = 1.0 / (1.0 + jnp.exp(-values))
    return logistic * (1.0 + values * (1.0 - logistic))


def kernel_body(
    sizes,
    field_hbm, cotangent_hbm, cosmology_hbm, lift_weight_hbm, lift_bias_hbm, style_hbm,
    style_bias_hbm, kernel_hbm, offset_hbm,
    grad, grad_packed, grad_rows, grad_style_t,
    field, cotangent, cosmology, lift_weight, lift_bias, style_t, style_bias, kernel, offset,
    fetch_sem, field_ext, up_ext, field_taps, up_taps, edge_out, edge_in, w_fwd, w_bwd, packed, field_rows, cot, turned_back, held, up_turned,
    share, from_z, part_z, from_xy, total,
    xy_send, xy_recv, z_send, z_recv, rz_send, rz_recv, rxy_send, rxy_recv, g_send, g_recv,
):
    nx, ny, nz = sizes
    C, CX, CY, CZ = field.shape
    EY = CY + 2
    taps = kernel.shape[0]
    per = CZ // C
    tiles = (taps + per) // per
    fetches = [
        pltpu.make_async_copy(source, there, fetch_sem.at[k])
        for k, (source, there) in enumerate(
            zip(
                (field_hbm, kernel_hbm, cosmology_hbm, lift_weight_hbm, lift_bias_hbm, style_hbm,
                 style_bias_hbm, offset_hbm, cotangent_hbm),
                (field, kernel, cosmology, lift_weight, lift_bias, style_t, style_bias, offset,
                 cotangent),
            )
        )
    ]
    fetches[0].start()
    me_x, me_y, me_z = (lax.axis_index("gx"), lax.axis_index("gy"), lax.axis_index("gz"))

    def at(dx=0, dy=0, dz=0):
        return (
            lax.rem(me_x + (dx + nx), nx) if dx else me_x,
            lax.rem(me_y + (dy + ny), ny) if dy else me_y,
            lax.rem(me_z + (dz + nz), nz) if dz else me_z,
        )

    plane_xy = [(dx, dy) for dx in range(nx) for dy in range(ny) if (dx, dy) != (0, 0)]
    plane_yz = [(dy, dz) for dy in range(ny) for dz in range(nz) if (dy, dz) != (0, 0)]
    edge_dx = (0, 1) if nx == 2 else (-1, 0, 1)
    corners = [(dx, dy, dz) for dz in (1, -1) for dx in edge_dx for dy in (-1, 0, 1)]
    steps = {}
    for dx, dy, dz in (
        [(dx, dy, 0) for dx, dy in SIDES + tuple(plane_xy)]
        + [(0, dy, dz) for dy, dz in plane_yz]
        + corners
    ):
        steps[(dx % nx, dy % ny, dz % nz)] = True
    partners = [at(*step) for step in steps]
    barrier = pltpu.get_barrier_semaphore()
    for partner in partners:
        pl.semaphore_signal(barrier, inc=1, device_id=partner, device_id_type=MESH)
    for fetch in fetches[1:]:
        fetch.start()
    sent = []

    def launch(copies):
        for copy in copies:
            copy.start()
        sent.extend(copies)

    def remote(src, dst, send, recv, device):
        return pltpu.make_async_remote_copy(
            src_ref=src, dst_ref=dst, send_sem=send, recv_sem=recv, device_id=device,
            device_id_type=MESH,
        )

    def span(step, count, first):
        if step == 0:
            return pl.ds(first, count), pl.ds(1, count)
        if step > 0:
            return pl.ds(first + count - 1, 1), pl.ds(0, 1)
        return pl.ds(first, 1), pl.ds(count + 1, 1)

    def side_copies(which, ext, near):
        copies = []
        for at_side, (dx, dy) in enumerate(SIDES):
            if (dx == 0) == near:
                sx, tx = span(dx, CX, 1)
                sy, ty = span(dy, CY, 1)
                copies.append(
                    remote(ext.at[sx, sy], ext.at[tx, ty], xy_send.at[which, at_side],
                           xy_recv.at[which, at_side], at(dx, dy))
                )
        return copies

    lanes = lax.broadcasted_iota(jnp.int32, (C, CZ), 1)
    group = lax.div(lanes, 2)

    def edge_copies(which, near):
        return [
            remote(edge_out.at[which],
                   edge_in.at[which, 0 if dz > 0 else 1, 1 - dx, 1 - dy],
                   z_send.at[which, k], z_recv.at[which, k], at(dx, dy, dz))
            for k, (dx, dy, dz) in enumerate(corners)
            if (dx == 0) == near
        ]

    def exchange(which, ext):
        near = side_copies(which, ext, True) + edge_copies(which, True)
        far = side_copies(which, ext, False) + edge_copies(which, False)
        launch(far + near)
        return near, far

    def pack_edges(which, ext):
        edges = jnp.zeros((C, CZ), jnp.float32)
        for x in range(CX):
            for y in range(CY):
                row = x * CY + y
                rolled = pltpu.roll(ext[x + 1, y + 1].astype(jnp.float32), 1 + 2 * row, 1)
                edges = jnp.where(group == row, rolled, edges)
        edge_out[which] = edges.astype(jnp.bfloat16)

    def build_taps(which, ext, out, p, place_x, x):
        tiles_at = {}
        for y in range(EY):
            place_y, source_y = (0, CY - 1) if y == 0 else (2, 0) if y == EY - 1 else (1, y - 1)
            if place_y not in tiles_at:
                before, after = (
                    edge_in[which, side, place_x, place_y].astype(jnp.float32) for side in (0, 1)
                )
                tiles_at[place_y] = jnp.where(lanes % 2 == 0, before, after)
            row = x * CY + source_y
            mid = ext[p, y]
            wide = mid.astype(jnp.float32)
            rim = pltpu.roll(tiles_at[place_y], CZ - 1 - 2 * row, 1)
            low = pltpu.roll(jnp.where(lanes == CZ - 1, rim, wide), 1, 1)
            high = pltpu.roll(jnp.where(lanes == 0, rim, wide), CZ - 1, 1)
            out[p, y, 0:C] = low.astype(jnp.bfloat16)
            out[p, y, C : 2 * C] = mid
            out[p, y, 2 * C : 3 * C] = high.astype(jnp.bfloat16)

    def build_near(which, ext, out):
        def plane(x, carry):
            build_taps(which, ext, out, x + 1, 1, x)
            return carry

        lax.fori_loop(0, CX, plane, 0)

    def build_far(which, ext, out):
        build_taps(which, ext, out, 0, 0, CX - 1)
        build_taps(which, ext, out, CX + 1, 0 if nx == 2 else 2, 0)

    def columns(source, p, y):
        return jnp.concatenate(
            [source[p, pl.ds(y + k, 3)].reshape(9 * C, CZ) for k in range(2)], axis=1
        )

    near_planes, far_planes = range(1, CX + 1), (0, CX + 1)

    def convolve(weights, source, y, planes, results):
        for p in planes:
            taken = [a for a in range(3) if 0 <= p - a < CX]
            product = jnp.dot(weights[taken[0] * C : (taken[-1] + 1) * C, :],
                              columns(source, p, y), preferred_element_type=jnp.float32)
            for k, a in enumerate(taken):
                term = product[k * C : (k + 1) * C]
                results[p - a] = term if results[p - a] is None else results[p - a] + term
        return results

    def line(x, y):
        return pl.ds(x * CY + y, C, stride=CX * CY)

    fetches[0].wait()
    field_rows[...] = field[...].astype(jnp.float32).reshape(C * CX * CY, CZ)
    for x in range(CX):
        for y in range(CY):
            field_ext[x + 1, y + 1] = field_rows[line(x, y), :].astype(jnp.bfloat16)
    pack_edges(0, field_ext)
    pl.semaphore_wait(barrier, len(partners))
    field_near, field_far = exchange(0, field_ext)
    for fetch in fetches[1:]:
        fetch.wait()

    eye = lax.broadcasted_iota(jnp.int32, (C, C), 0) == lax.broadcasted_iota(jnp.int32, (C, C), 1)

    def to_row(column):
        return jnp.sum(jnp.where(eye, column, 0.0), axis=0, keepdims=True)

    def to_column(row):
        return jnp.sum(jnp.where(eye, row, 0.0), axis=1, keepdims=True)

    lifted = lift_bias[...]
    for k in range(lift_weight.shape[0]):
        lifted = lifted + cosmology[0:1, k : k + 1] * lift_weight[k : k + 1, :]
    hidden = lifted / (1.0 + jnp.exp(-lifted))
    styles_column = (
        jnp.sum(style_t[...] * hidden, axis=1, keepdims=True) + to_column(style_bias[...]) + 1.0
    )
    styles = to_row(styles_column)
    styles_wide = jnp.concatenate([styles] * per, axis=1)
    squares = jnp.zeros((C, CZ), jnp.float32)
    for j in range(tiles):
        members = [
            kernel[per * j + k] if per * j + k < taps else jnp.zeros((C, C), jnp.float32)
            for k in range(per)
        ]
        tile = jnp.concatenate(members, axis=1)
        packed[j] = tile
        modded = tile * styles_wide
        squares = squares + modded * modded
    inv_norm = lax.rsqrt(jnp.sum(squares, axis=1, keepdims=True) + demod_eps)
    turned = []
    for j in range(tiles):
        flat = (packed[j] * styles_wide * inv_norm).T
        turned += [flat[k * C : (k + 1) * C] for k in range(per)]
    turned = turned[:taps][::-1]
    for a in range(3):
        taken = range(9 * a, 9 * a + 9)
        w_fwd[a * C : (a + 1) * C, :] = jnp.concatenate(
            [kernel[t] * styles * inv_norm for t in taken], axis=1
        ).astype(jnp.bfloat16)
        w_bwd[a * C : (a + 1) * C, :] = jnp.concatenate(
            [turned[t] for t in taken], axis=1
        ).astype(jnp.bfloat16)
    offset_column = to_column(offset[...])
    cot[...] = cotangent[...].astype(jnp.float32).reshape(C * CX * CY, CZ)

    for copy in field_near:
        copy.wait_recv()
    build_near(0, field_ext, field_taps)

    depth = taps * C

    edge_x = sorted({0, CX - 1})

    def finish(x, y, sums):
        above = jnp.concatenate([cot[line(x, y), :], cot[line(x, y + 1), :]], axis=1)
        upstream = (above * silu_slope(sums + offset_column)).astype(jnp.bfloat16)
        up_ext[x + 1, y + 1] = upstream[:, :CZ]
        up_ext[x + 1, y + 2] = upstream[:, CZ:]

    def forward_near(at_pair, carry):
        y = 2 * at_pair
        results = convolve(w_fwd, field_taps, y, near_planes, [None] * CX)
        for x, sums in enumerate(results):
            if x in edge_x:
                held[x, at_pair] = sums
            else:
                finish(x, y, sums)
        return carry

    def forward_far(at_pair, carry):
        y = 2 * at_pair
        results = [held[x, at_pair] if x in edge_x else None for x in range(CX)]
        results = convolve(w_fwd, field_taps, y, far_planes, results)
        for x in edge_x:
            finish(x, y, results[x])
        return carry

    lax.fori_loop(0, CY // 2, forward_near, 0)
    for copy in field_far:
        copy.wait_recv()
    build_far(0, field_ext, field_taps)
    lax.fori_loop(0, CY // 2, forward_far, 0)

    offsets = jnp.zeros((C, CZ), jnp.float32)
    blank = [jnp.zeros((C, CZ), jnp.float32)] * (per - CX)
    for y in range(CY):
        ups = [up_ext[x + 1, y + 1].astype(jnp.float32) for x in range(CX)]
        for up in ups:
            offsets = offsets + up
        up_turned[y * CZ : (y + 1) * CZ, :] = jnp.concatenate(ups + blank, axis=0).T.astype(
            jnp.bfloat16
        )
    block = lax.div(lax.broadcasted_iota(jnp.int32, (9 * C, CZ), 1), C)
    products = []
    for p in range(CX + 2):
        streamed = jnp.concatenate(
            [field_taps[p, y : y + 3].reshape(9 * C, CZ) for y in range(CY)], axis=1
        )
        products.append(jnp.dot(streamed, up_turned[...], preferred_element_type=jnp.float32))
    merged = jnp.zeros((9 * C, CZ), jnp.float32)
    for a in range(3):
        chosen = products[a]
        for x in range(1, CX):
            chosen = jnp.where(block == x, products[a + x], chosen)
        shift = CZ // 2
        while shift >= C:
            chosen = chosen + pltpu.roll(chosen, shift, 1)
            shift //= 2
        merged = jnp.where(block == a, chosen, merged)
    flats = [merged[k : min(k + CZ, 9 * C)].T for k in range(0, 9 * C, CZ)]
    sums = jnp.concatenate(
        [flat[a * C : (a + 1) * C] for a in range(3) for flat in flats], axis=1
    )
    offset_sum = jnp.sum(offsets, axis=1, keepdims=True)
    for j in range(share.shape[0] // C):
        if (j + 1) * CZ <= depth:
            tile = sums[:, j * CZ : (j + 1) * CZ]
        elif j < tiles:
            used = depth - j * CZ
            tile = jnp.concatenate(
                [sums[:, j * CZ : depth], jnp.broadcast_to(offset_sum, (C, CZ - used))], axis=1
            )
        else:
            tile = jnp.zeros((C, CZ), jnp.float32)
        share[j * C : (j + 1) * C] = tile.astype(jnp.bfloat16)

    rows_z = share.shape[0] // nz
    rows_y = rows_z // ny

    def rows_at(base, count):
        return pl.ds(pl.multiple_of(base, 16), count)

    reduce_z = []
    for k in range(1, nz):
        there = at(dz=k)
        reduce_z.append(remote(share.at[rows_at(there[2] * rows_z, rows_z)], from_z.at[k - 1],
                               rz_send.at[k - 1], rz_recv.at[k - 1], there))
    launch(reduce_z)

    pack_edges(1, up_ext)
    up_near, up_far = exchange(1, up_ext)

    for copy in reduce_z:
        copy.wait_recv()
    mine = share[rows_at(me_z * rows_z, rows_z), :].astype(jnp.float32)
    for k in range(1, nz):
        mine = mine + from_z[k - 1].astype(jnp.float32)
    part_z[...] = mine.astype(jnp.bfloat16)
    my_slot = me_x * ny + me_y
    reduce_xy = []
    for k, (dx, dy) in enumerate(plane_xy):
        there = at(dx, dy)
        reduce_xy.append(remote(part_z.at[rows_at(there[1] * rows_y, rows_y)], from_xy.at[my_slot],
                                rxy_send.at[k], rxy_recv.at[k], there))
    launch(reduce_xy)
    from_xy[my_slot] = part_z[rows_at(me_y * rows_y, rows_y), :]

    for copy in up_near:
        copy.wait_recv()
    build_near(1, up_ext, up_taps)

    def backward_near(at_pair, carry):
        y = 2 * at_pair
        for x, sums in enumerate(convolve(w_bwd, up_taps, y, near_planes, [None] * CX)):
            held[x, at_pair] = sums
        return carry

    def backward_far(at_pair, carry):
        y = 2 * at_pair
        results = [held[x, at_pair] for x in range(CX)]
        for x, sums in enumerate(convolve(w_bwd, up_taps, y, far_planes, results)):
            turned_back[line(x, y), :] = sums[:, :CZ]
            turned_back[line(x, y + 1), :] = sums[:, CZ:]
        return carry

    lax.fori_loop(0, CY // 2, backward_near, 0)

    for copy in reduce_xy:
        copy.wait_recv()
    mine = from_xy[0].astype(jnp.float32)
    for k in range(1, nx * ny):
        mine = mine + from_xy[k].astype(jnp.float32)
    own = rows_at(me_z * rows_z + me_y * rows_y, rows_y)
    total[own, :] = mine.astype(jnp.bfloat16)
    gather = [
        remote(total.at[own], total.at[own], g_send.at[k], g_recv.at[k], at(0, dy, dz))
        for k, (dy, dz) in enumerate(plane_yz)
    ]
    launch(gather)
    for copy in up_far:
        copy.wait_recv()
    build_far(1, up_ext, up_taps)
    lax.fori_loop(0, CY // 2, backward_far, 0)
    grad[...] = turned_back[...].reshape(grad.shape).astype(jnp.bfloat16)
    for copy in gather:
        copy.wait_recv()

    last = taps - per * (tiles - 1)
    projected = jnp.zeros((C, CZ), jnp.float32)
    sum_tiles, modded_tiles = [], []
    for j in range(tiles):
        tile = total[j * C : (j + 1) * C, :].astype(jnp.float32)
        if j == tiles - 1:
            offset_row = to_row(tile[:, last * C : last * C + 1])
            tile = jnp.where(lanes < last * C, tile, 0.0)
        modded = packed[j] * styles_wide
        projected = projected + tile * modded
        sum_tiles.append(tile)
        modded_tiles.append(modded)
    projected = jnp.sum(projected, axis=1, keepdims=True)
    scale = inv_norm * inv_norm * projected
    raws = []
    square = jnp.zeros((C, CZ), jnp.float32)
    along = jnp.zeros((C, CZ), jnp.float32)
    for j in range(tiles):
        mod_grad = inv_norm * (sum_tiles[j] - modded_tiles[j] * scale)
        raw = mod_grad * styles_wide
        along = along + mod_grad * packed[j]
        square = square + raw * raw
        raws.append(raw)
    along = jnp.sum(along, axis=0, keepdims=True)
    styles_grad = along[:, 0:C]
    for k in range(1, per):
        styles_grad = styles_grad + along[:, k * C : (k + 1) * C]
    styles_grad_column = to_column(styles_grad)
    hidden_grad = jnp.sum(style_t[...] * styles_grad_column, axis=0, keepdims=True)
    lifted_grad = hidden_grad * silu_slope(lifted)
    style_raw = styles_grad_column * hidden
    lift_raws = [
        cosmology[0:1, k : k + 1] * lifted_grad for k in range(lift_weight.shape[0])
    ]

    def sum_all(values):
        return jnp.sum(jnp.sum(values, axis=1, keepdims=True), axis=0, keepdims=True)

    square_sum = sum_all(square)
    for member in [offset_row, lifted_grad, style_raw, styles_grad] + lift_raws:
        square_sum = square_sum + sum_all(member * member)
    entries = taps * C * C + 2 * C + (1 + lift_weight.shape[0] + C) * lifted.shape[1]
    factor = jnp.minimum(1.0, lax.rsqrt(square_sum / entries + clip_eps))
    for j in range(tiles):
        grad_packed[j] = raws[j] * factor
    for copy in sent:
        copy.wait_send()
    grad_style_t[...] = style_raw * factor
    wide = lifted.shape[1]
    small = jnp.concatenate([offset_row, styles_grad], axis=1)
    grad_rows[0:1, 0 : 2 * C] = small * factor
    grad_rows[1:2, :] = lifted_grad * factor
    for k in range(lift_weight.shape[0]):
        grad_rows[k + 2 : k + 3, :] = lift_raws[k] * factor


def hand_out(
    grad_in, grad_packed, grad_rows, grad_style_in,
    grad, grad_kernel, grad_offset, grad_lift, grad_liftbias, grad_style_t, grad_stylebias,
):
    C = grad_packed.shape[1]
    per = grad_packed.shape[2] // C
    grad[...] = grad_in[...]
    for t in range(grad_kernel.shape[0]):
        k = t % per
        grad_kernel[t] = grad_packed[t // per][:, k * C : (k + 1) * C]
    grad_offset[...] = grad_rows[0:1, 0:C]
    grad_stylebias[...] = grad_rows[0:1, C : 2 * C]
    grad_liftbias[...] = grad_rows[1:2, :]
    grad_lift[...] = grad_rows[2 : 2 + grad_lift.shape[0], :]
    grad_style_t[...] = grad_style_in[...]


def body(
    sizes, field, cotangent, cosmology, lift_weight, lift_bias, style_weight, style_bias, kernel,
    offset,
):
    nx, ny, nz = sizes
    C, CX, CY, CZ = field.shape
    HID = lift_bias.shape[0]
    taps = kernel.shape[2] * kernel.shape[3] * kernel.shape[4]
    per = CZ // C
    tiles = (taps + per) // per
    unit = nz * ny * 16
    rows = -(-tiles * C // unit) * unit
    f32, bf16 = jnp.float32, jnp.bfloat16
    dma = pltpu.SemaphoreType.DMA
    vmem = pl.BlockSpec(memory_space=pltpu.VMEM)
    results = pl.pallas_call(
        functools.partial(kernel_body, sizes),
        out_shape=[
            jax.ShapeDtypeStruct(field.shape, bf16),
            jax.ShapeDtypeStruct((tiles, C, CZ), f32),
            jax.ShapeDtypeStruct((8, HID), f32),
            jax.ShapeDtypeStruct((C, HID), f32),
        ],
        in_specs=[pl.BlockSpec(memory_space=pltpu.HBM)] * 9,
        out_specs=[vmem] * 4,
        scratch_shapes=[
            pltpu.VMEM(field.shape, bf16),
            pltpu.VMEM(field.shape, bf16),
            pltpu.VMEM((1, cosmology.shape[0]), f32),
            pltpu.VMEM(lift_weight.shape, f32),
            pltpu.VMEM((1, HID), f32),
            pltpu.VMEM((C, HID), f32),
            pltpu.VMEM((1, C), f32),
            pltpu.VMEM((taps, C, C), f32),
            pltpu.VMEM((1, C), f32),
            dma((9,)),
            pltpu.VMEM((CX + 2, CY + 2, C, CZ), bf16),
            pltpu.VMEM((CX + 2, CY + 2, C, CZ), bf16),
            pltpu.VMEM((CX + 2, CY + 2, 3 * C, CZ), bf16),
            pltpu.VMEM((CX + 2, CY + 2, 3 * C, CZ), bf16),
            pltpu.VMEM((2, C, CZ), bf16),
            pltpu.VMEM((2, 2, 3, 3, C, CZ), bf16),
            pltpu.VMEM((3 * C, 9 * C), bf16),
            pltpu.VMEM((3 * C, 9 * C), bf16),
            pltpu.VMEM((tiles, C, CZ), f32),
            pltpu.VMEM((C * CX * CY, CZ), f32),
            pltpu.VMEM((C * CX * CY, CZ), f32),
            pltpu.VMEM((C * CX * CY, CZ), f32),
            pltpu.VMEM((CX, CY // 2, C, 2 * CZ), f32),
            pltpu.VMEM((CY * CZ, CZ), bf16),
            pltpu.VMEM((rows, CZ), bf16),
            pltpu.VMEM((nz - 1, rows // nz, CZ), bf16),
            pltpu.VMEM((rows // nz, CZ), bf16),
            pltpu.VMEM((nx * ny, rows // nz // ny, CZ), bf16),
            pltpu.VMEM((rows, CZ), bf16),
            dma((2, 8)), dma((2, 8)), dma((2, 18)), dma((2, 18)),
            dma((nz - 1,)), dma((nz - 1,)), dma((nx * ny - 1,)), dma((nx * ny - 1,)),
            dma((ny * nz - 1,)), dma((ny * nz - 1,)),
        ],
        compiler_params=pltpu.CompilerParams(
            collective_id=0, has_side_effects=True, vmem_limit_bytes=60 * 1024 * 1024
        ),
    )(
        field,
        cotangent,
        cosmology[None],
        lift_weight,
        lift_bias[None],
        style_weight.T,
        style_bias[None],
        jnp.transpose(kernel, (2, 3, 4, 0, 1)).reshape(taps, C, C),
        offset[None],
    )
    grad, grad_kernel, grad_offset, grad_lift, grad_liftbias, grad_style_t, grad_stylebias = (
        pl.pallas_call(
            hand_out,
            out_shape=[
                jax.ShapeDtypeStruct(field.shape, bf16),
                jax.ShapeDtypeStruct((taps, C, C), f32),
                jax.ShapeDtypeStruct((1, C), f32),
                jax.ShapeDtypeStruct(lift_weight.shape, f32),
                jax.ShapeDtypeStruct((1, HID), f32),
                jax.ShapeDtypeStruct((C, HID), f32),
                jax.ShapeDtypeStruct((1, C), f32),
            ],
            in_specs=[vmem] * 4,
            out_specs=[vmem] * 7,
            compiler_params=pltpu.CompilerParams(vmem_limit_bytes=60 * 1024 * 1024),
        )(*results)
    )
    return (
        grad,
        jnp.transpose(grad_kernel.reshape(kernel.shape[2:] + (C, C)), (3, 4, 0, 1, 2)),
        grad_offset[0],
        grad_lift,
        grad_liftbias[0],
        grad_style_t.T,
        grad_stylebias[0],
    )


def solution(mesh):
    sizes = (mesh.shape["gx"], mesh.shape["gy"], mesh.shape["gz"])
    placed = P(None, "gx", "gy", "gz")
    return jax.shard_map(
        functools.partial(body, sizes),
        mesh=mesh,
        in_specs=(placed, placed, P(), P(), P(), P(), P(), P(), P()),
        out_specs=(placed, P(), P(), P(), P(), P(), P()),
        check_vma=False,
    )
```
